512 devices in a mesh: blk: 128 (over y_lo, z, x, core), grp: 4 (over y_hi).
Axes of the slice: x: 4, y: 8 (y_hi: 4, y_lo: 2; y = y_hi * 2 + y_lo), z: 8, core: 2. Of those that a mesh axis runs over, the one named last changes fastest.
Arguments:
- query_rows: bfloat16 [65536, 1024], P(('grp', 'blk')), parts along dimension 0, may hold values from -6 to 6
- key_rows: bfloat16 [65536, 1024], P(('grp', 'blk')), parts along dimension 0, may hold values from -6 to 6
- value_rows: bfloat16 [65536, 1024], P(('grp', 'blk')), parts along dimension 0, may hold values from -6 to 6
- gate_rows: bfloat16 [65536, 1024], P(('grp', 'blk')), parts along dimension 0, may hold values from -24 to 24
- segment: int32 [65536], P('grp'), parts along dimension 0, may hold values from 0 to 3, never falling along the last dimension, each value on 1 to 8192 neighbouring positions
- w_out: bfloat16 [1024, 1024], P('blk'), may hold values from -0.1875 to 0.1875
- cotangent: bfloat16 [65536, 1024], P(('grp', 'blk')), parts along dimension 0, may hold values from -6 to 6
Outputs:
- query_grad: bfloat16 [65536, 1024], P(('grp', 'blk')), parts along dimension 0
- key_grad: bfloat16 [65536, 1024], P(('grp', 'blk')), parts along dimension 0
- value_grad: bfloat16 [65536, 1024], P(('grp', 'blk')), parts along dimension 0
- gate_grad: bfloat16 [65536, 1024], P(('grp', 'blk')), parts along dimension 0
- w_grad: float32 [4096, 1024], P(('grp', 'blk')), parts along dimension 0
The draws below stay inside these ranges and needn't reach their ends.
There are 4 independent parts, one for each index of `grp`. The reference program is written for one: setup_inputs(seed, part) draws one part's arguments, and reference() takes and returns one part's arrays. A program takes and returns all parts, laid end to end along the dimension named above; an argument that names none is the same for every part. Nothing has to cross between parts.
Inputs may be any that keep to these rules, and one draw needn't show every extreme that they name: Segment numbers never fall along the events; every segment holds 1 to 8192 events, and one holds exactly 8192.
All inputs are finite; a program needn't handle non-finite values.
Results may differ from the reference program's by a relative error of at most 0.0058.
Values may be sent and summed in bfloat16 or wider, within the bound.
No kernel may reach another device: no remote copies, remote signals or barrier semaphores. Data moves between devices by JAX's collectives and lax.ppermute only.
A program may use at most 64 MiB of HBM per device.

```python
import math
import jax
import jax.numpy as jnp
import numpy as np
from jax import lax

D = 1024
DH = 128
REACH = 4
TOK_DEV = 128
TOKENS = 16384


def with_spikes(values, stream_key, source, target, shards_of, factor):
    owner, partner = [(jnp.arange(values.shape[position]) // (values.shape[position] // shards_of)).reshape([-1 if axis == position else 1 for axis in range(values.ndim)]) for position in (source, target)]
    chosen = jax.random.permutation(stream_key, shards_of)[partner]
    strong = (owner == chosen) | (owner == (partner + shards_of // 2) % shards_of)
    return jnp.where(strong, factor * values, values)


def block_scale(stream_key, extent, split, smallest, top_value):
    def one(position, parts):
        draws = jax.random.uniform(jax.random.fold_in(jax.random.fold_in(stream_key, 6), position), (parts,), jnp.float32, smallest / len(split), top_value / len(split))
        return jnp.repeat(jnp.exp(draws), extent[position] // parts).reshape((-1,) + (1,) * (len(extent) - position - 1))

    factor_of = one(*split[0])
    for cut in split[1:]:
        factor_of = factor_of * one(*cut)
    return factor_of


def split_up(count, total, reach, lean):
    loads = [(1 << 20) // math.isqrt(grade ** lean) + 1 for grade in range(2, count + 1)]
    rest, counts = total - reach - (count - 1), [1] * (count - 1)
    while rest > 0:
        movable = [i for i in range(count - 1) if counts[i] < reach]
        whole, remaining = sum([loads[i] for i in movable]), rest
        for i in movable:
            addition = min(reach - counts[i], max(1, remaining * loads[i] // whole), rest)
            counts[i] = counts[i] + addition
            rest = rest - addition
    return np.array([reach] + counts)


def ragged_sizes(own_key, count, total, limit, lean):
    if count == 2:
        one = jax.random.randint(own_key, (), max(1, total - limit), min(limit, total - 1) + 1)
        return jnp.stack([one, total - one])
    sizes = jnp.asarray(split_up(count, total, limit, lean), jnp.int32)
    twos = (count - 1) // 2
    giver, receiver = sizes[1:1 + 2 * twos:2], sizes[2:2 + 2 * twos:2]
    slack = jnp.minimum(giver - 1, limit - receiver)
    moved = jax.random.randint(jax.random.fold_in(own_key, 1), (twos,), 0, 1 << 20) % (slack + 1)
    sizes = sizes.at[1:1 + 2 * twos:2].set(giver - moved).at[2:2 + 2 * twos:2].set(receiver + moved)
    return sizes[jax.random.permutation(jax.random.fold_in(own_key, 2), count)]


def scatter_about(stream_key, shape, width, reach, split=(), kind=jnp.bfloat16):
    result = width * jax.random.normal(stream_key, shape, jnp.float32)
    if split:
        result = result * block_scale(stream_key, shape, split, -0.22, 0.18)
    return jnp.clip(result, -reach, reach).astype(kind)


def heavy_noise(own_key, extent, deviation, reach, shards, heavy, held_as=jnp.bfloat16):
    entries = deviation * jax.random.normal(own_key, extent, jnp.float32)
    if shards:
        entries = entries * block_scale(own_key, extent, shards, -0.22, 0.18)
    return jnp.clip(with_spikes(entries, jax.random.fold_in(own_key, 3), *heavy), -reach, reach).astype(held_as)


def setup_inputs(seed: int = 0, part: int = 0) -> dict:
    key_list = jax.random.split(jax.random.key(seed), 8)
    part_keys = jax.random.split(jax.random.fold_in(key_list[7], part), 8)
    query_rows = scatter_about(part_keys[0], (TOKENS, D), 1.0, 6.0, ((0, 128),))
    key_rows = scatter_about(part_keys[1], (TOKENS, D), 1.0, 6.0, ((0, 128),))
    value_rows = scatter_about(part_keys[2], (TOKENS, D), 1.0, 6.0, ((0, 128),))
    gate_rows = heavy_noise(part_keys[3], (TOKENS, D), 1.0, 24.0, ((0, 128),), (0, 1, 128, 5.5))
    segment = jnp.searchsorted(jnp.cumsum(ragged_sizes(part_keys[4], 4, TOKENS, TOKENS // 2, 2)), jnp.arange(TOKENS), side="right").astype(jnp.int32)
    w_out = scatter_about(key_list[5], (D, D), D ** -0.5, 0.1875, ((0, 128),))
    cotangent = scatter_about(part_keys[6], (TOKENS, D), 1.0, 6.0, ((0, 128),))
    return dict(query_rows=query_rows, key_rows=key_rows, value_rows=value_rows, gate_rows=gate_rows, segment=segment, w_out=w_out, cotangent=cotangent)


def reference(query_rows, key_rows, value_rows, gate_rows, segment, w_out, cotangent):
    scale = DH ** (-0.5)
    span = REACH * TOK_DEV
    lead = (REACH - 1) * TOK_DEV
    heads = D // DH
    blocks = TOKENS // TOK_DEV

    def padded(array):
        return jnp.concatenate([jnp.zeros((lead,) + array.shape[1:], array.dtype), array], 0)
    key_pad = padded(key_rows)
    value_pad = padded(value_rows)
    segment_pad = padded(segment)
    local = jnp.arange(TOK_DEV, dtype=jnp.int32)
    window = jnp.arange(span, dtype=jnp.int32)

    def pieces(index):
        start = (index * TOK_DEV).astype(jnp.int32)
        queries = lax.dynamic_slice_in_dim(query_rows, start, TOK_DEV, 0).astype(jnp.float32).reshape(TOK_DEV, heads, DH)
        keyed = lax.dynamic_slice_in_dim(key_pad, start, span, 0).astype(jnp.float32).reshape(span, heads, DH)
        valued = lax.dynamic_slice_in_dim(value_pad, start, span, 0).astype(jnp.float32).reshape(span, heads, DH)
        seg_query = lax.dynamic_slice_in_dim(segment, start, TOK_DEV, 0)
        seg_key = lax.dynamic_slice_in_dim(segment_pad, start, span, 0)
        query_pos = start + local
        key_pos = start - lead + window
        allowed = (seg_query[:, None] == seg_key[None, :]) & (key_pos[None, :] <= query_pos[:, None]) & (key_pos[None, :] >= 0) & (key_pos[None, :] >= query_pos[:, None] - lead)
        scores = jnp.einsum('qhd,khd->hqk', queries, keyed) * scale
        return (start, queries, keyed, valued, allowed.astype(jnp.float32), scores)

    def forward(index):
        start, queries, keyed, valued, allowed, scores = pieces(index)
        weights = lax.optimization_barrier((jax.nn.sigmoid(scores) * scores * allowed[None]).astype(jnp.bfloat16)).astype(jnp.float32)
        return jnp.einsum('hqk,khd->qhd', weights, valued).reshape(TOK_DEV, D)
    attended = lax.map(forward, jnp.arange(blocks, dtype=jnp.int32)).reshape(TOKENS, D)
    mean = lax.optimization_barrier(jnp.mean(attended, axis=-1, keepdims=True))
    centred = attended - mean
    rstd = lax.rsqrt(lax.optimization_barrier(jnp.mean(centred * centred, axis=-1, keepdims=True)) + 1e-05)
    normed = centred * rstd
    gate = gate_rows.astype(jnp.float32)
    hidden = (normed * gate).astype(jnp.bfloat16)
    w_grad = jnp.dot(hidden.T, cotangent, preferred_element_type=jnp.float32)
    hidden_grad = jnp.dot(cotangent, w_out.T, preferred_element_type=jnp.float32)
    gate_grad = (hidden_grad * normed).astype(jnp.bfloat16)
    normed_grad = hidden_grad * gate
    attended_grad = rstd * (normed_grad - lax.optimization_barrier(jnp.mean(normed_grad, axis=-1, keepdims=True)) - normed * lax.optimization_barrier(jnp.mean(normed_grad * normed, axis=-1, keepdims=True)))
    upstream = lax.optimization_barrier(attended_grad.astype(jnp.bfloat16))

    def backward(carry, index):
        key_buffer, value_buffer = carry
        start, queries, keyed, valued, allowed, scores = pieces(index)
        upper = lax.dynamic_slice_in_dim(upstream, start, TOK_DEV, 0).astype(jnp.float32).reshape(TOK_DEV, heads, DH)
        sigma = jax.nn.sigmoid(scores)
        weights = lax.optimization_barrier((sigma * scores * allowed[None]).astype(jnp.bfloat16)).astype(jnp.float32)
        weight_grad = jnp.einsum('qhd,khd->hqk', upper, valued)
        score_grad = lax.optimization_barrier((weight_grad * allowed[None] * sigma * (1.0 + scores * (1.0 - sigma))).astype(jnp.bfloat16)).astype(jnp.float32)
        query_part = jnp.einsum('hqk,khd->qhd', score_grad, keyed).reshape(TOK_DEV, D) * scale
        key_part = jnp.einsum('hqk,qhd->khd', score_grad, queries).reshape(span, D)
        value_part = jnp.einsum('hqk,qhd->khd', weights, upper).reshape(span, D)
        key_buffer = lax.dynamic_update_slice_in_dim(key_buffer, lax.dynamic_slice_in_dim(key_buffer, start, span, 0) + key_part, start, 0)
        value_buffer = lax.dynamic_update_slice_in_dim(value_buffer, lax.dynamic_slice_in_dim(value_buffer, start, span, 0) + value_part, start, 0)
        return ((key_buffer, value_buffer), query_part)
    empty = jnp.zeros((lead + TOKENS, D), jnp.float32)
    (key_buffer, value_buffer), query_parts = lax.scan(backward, (empty, empty), jnp.arange(blocks, dtype=jnp.int32))
    query_grad = query_parts.reshape(TOKENS, D).astype(jnp.bfloat16)
    key_grad = (key_buffer[lead:] * scale).astype(jnp.bfloat16)
    value_grad = value_buffer[lead:].astype(jnp.bfloat16)
    return (query_grad, key_grad, value_grad, gate_grad, w_grad)
```

```python
import jax
import jax.numpy as jnp
import numpy as np
from jax import lax
from jax.sharding import Mesh, PartitionSpec as P

DH = 128
REACH = 4
NY, NZ, NX, NC = 2, 8, 4, 2
BLK = ("y", "z", "x", "c")
ROW = ("x", "c")
COL = ("y", "z")


def shift(value, steps, sources=None):
    count = NY * NZ * NX * NC
    pairs = [(s, s + steps) for s in (sources or range(count)) if 0 <= s + steps < count]
    return lax.ppermute(value, BLK, pairs)


def ring(value, axis, size, steps):
    return lax.ppermute(value, axis, [(s, (s + steps) % size) for s in range(size)])


def swap(value):
    return ring(value, "c", NC, 1)


def body(query_rows, key_rows, value_rows, gate_rows, segment, w_out, cotangent):
    rows, width = query_rows.shape
    heads = width // DH
    scale = DH ** (-0.5)
    total = segment.shape[0]
    reach_rows = (REACH - 1) * rows
    core = lax.axis_index("c")
    xpos = lax.axis_index("x")
    device = lax.axis_index(BLK)
    own_start = device * rows
    local = jnp.arange(rows, dtype=jnp.int32)
    even = core == 0
    groups, members = NY * NZ, NX * NC
    part = rows // groups

    natural = np.arange(width)
    unit = w_out.shape[0]
    placed = (natural // unit % members) * (groups * unit) + natural // (unit * members) * unit + natural % unit
    to_placed = jnp.asarray(np.eye(width, dtype=np.float32)[:, np.argsort(placed)], jnp.bfloat16)

    def pair(mine, other):
        return jnp.where(even, mine, other), jnp.where(even, other, mine)

    kv = jnp.concatenate([key_rows, value_rows], 0)
    odd_sources = range(1, NY * NZ * NX * NC, 2)
    kv_chip = shift(kv, 2)
    kv_far = shift(kv, 3, odd_sources)
    qkv_sib = swap(jnp.concatenate([query_rows, kv], 0))
    q_sib, kv_sib = qkv_sib[:rows], qkv_sib[rows:]
    kv_cross = swap(kv_chip)
    memory = [
        kv,
        jnp.where(even, kv_cross, kv_sib),
        kv_chip,
        jnp.where(even, kv_far, kv_cross),
    ]

    rel = jnp.stack([cotangent] + [ring(cotangent, "x", NX, k) for k in range(1, NX)])
    rel_other = swap(rel)
    first, second = pair(rel, rel_other)
    cot_rel = jnp.stack([first, second], 1)
    order = (xpos - jnp.arange(NX)) % NX
    cot_abs = jnp.take(cot_rel, order, axis=0).reshape(members * rows, width)
    w_sub = lax.all_to_all(
        jnp.broadcast_to(w_out[None], (groups,) + w_out.shape), COL, 0, 0, tiled=True
    ).reshape(groups * unit, width)
    hg = jnp.einsum("te,de->td", cot_abs, w_sub, preferred_element_type=jnp.float32)
    hg = lax.all_to_all(hg.astype(jnp.bfloat16).reshape(members, rows, groups * unit), ROW, 0, 0, tiled=True)
    hg = hg.transpose(1, 0, 2).reshape(rows, width)
    hidden_grad = jnp.einsum("tp,dp->td", hg, to_placed, preferred_element_type=jnp.float32)

    def split(array):
        return array.reshape(rows, heads, DH)

    def segment_slice(start):
        return lax.dynamic_slice_in_dim(segment, jnp.clip(start, 0, total - rows), rows, 0)

    def block_mask(query_start, key_start):
        query_pos = query_start + local
        key_pos = key_start + local
        same = segment_slice(query_start)[:, None] == segment_slice(key_start)[None, :]
        valid = (
            (key_pos[None, :] <= query_pos[:, None])
            & (key_pos[None, :] >= 0)
            & (query_pos[:, None] < total)
            & (key_pos[None, :] >= query_pos[:, None] - reach_rows)
        )
        return (same & valid).astype(jnp.float32)

    def scores_of(queries, keyed):
        return (
            jnp.einsum("qhd,khd->hqk", queries, keyed, preferred_element_type=jnp.float32) * scale
        )

    queries = split(query_rows)
    attended = jnp.zeros((rows, heads, DH), jnp.float32)
    back = []
    for offset in range(REACH):
        keyed = split(memory[offset][:rows])
        valued = split(memory[offset][rows:])
        allowed = block_mask(own_start, own_start - offset * rows)
        scores = scores_of(queries, keyed)
        weights = (jax.nn.sigmoid(scores) * scores * allowed[None]).astype(jnp.bfloat16)
        attended = attended + jnp.einsum(
            "hqk,khd->qhd", weights, valued, preferred_element_type=jnp.float32
        )
        back.append((keyed, valued, allowed))
    attended = attended.reshape(rows, width)
    mean = jnp.mean(attended, axis=-1, keepdims=True)
    centred = attended - mean
    rstd = lax.rsqrt(jnp.mean(centred * centred, axis=-1, keepdims=True) + 1e-05)
    normed = centred * rstd
    gate = gate_rows.astype(jnp.float32)
    hidden = (normed * gate).astype(jnp.bfloat16)
    hidden = jnp.einsum("td,dp->tp", hidden, to_placed, preferred_element_type=jnp.float32)
    hidden = hidden.astype(jnp.bfloat16).reshape(rows, members, groups * unit).transpose(1, 0, 2)
    hidden_all = lax.all_to_all(hidden, ROW, 0, 0, tiled=True).reshape(members * rows, groups * unit)
    w_part = jnp.einsum("tr,te->re", hidden_all, cot_abs, preferred_element_type=jnp.float32)
    w_parts = lax.all_to_all(w_part.reshape(groups, unit, width), COL, 0, 0, tiled=True)
    w_grad = jnp.sum(w_parts, axis=0)

    gate_grad = (hidden_grad * normed).astype(jnp.bfloat16)
    normed_grad = hidden_grad * gate
    attended_grad = rstd * (
        normed_grad
        - jnp.mean(normed_grad, axis=-1, keepdims=True)
        - normed * jnp.mean(normed_grad * normed, axis=-1, keepdims=True)
    )
    upstream = attended_grad.astype(jnp.bfloat16)

    uq = jnp.concatenate([upstream, query_rows], 0)
    even_sources = range(0, NY * NZ * NX * NC, 2)
    uq_chip = shift(uq, -2)
    uq_far = shift(uq, -3, even_sources)
    u_sib = swap(upstream)
    uq_cross = swap(uq_chip)
    uq_sib = jnp.concatenate([u_sib, q_sib], 0)
    later = [
        uq,
        jnp.where(even, uq_sib, uq_cross),
        uq_chip,
        jnp.where(even, uq_cross, uq_far),
    ]

    upper = split(upstream)
    query_grad = jnp.zeros((rows, heads, DH), jnp.float32)
    key_total = jnp.zeros((rows, heads, DH), jnp.float32)
    value_total = jnp.zeros((rows, heads, DH), jnp.float32)

    def grads(pair_queries, pair_upper, keyed, valued, allowed):
        pair_scores = scores_of(pair_queries, keyed)
        sigma = jax.nn.sigmoid(pair_scores)
        weights = (sigma * pair_scores * allowed[None]).astype(jnp.bfloat16)
        weight_grad = jnp.einsum("qhd,khd->hqk", pair_upper, valued, preferred_element_type=jnp.float32)
        score_grad = (
            weight_grad * allowed[None] * sigma * (1.0 + pair_scores * (1.0 - sigma))
        ).astype(jnp.bfloat16)
        return weights, score_grad

    for offset in range(REACH):
        keyed, valued, allowed = back[offset]
        weights, score_grad = grads(queries, upper, keyed, valued, allowed)
        query_grad = query_grad + jnp.einsum(
            "hqk,khd->qhd", score_grad, keyed, preferred_element_type=jnp.float32
        )
        if offset:
            pair_upper = split(later[offset][:rows])
            pair_queries = split(later[offset][rows:])
            allowed = block_mask(own_start + offset * rows, own_start)
            keyed, valued, _ = back[0]
            weights, score_grad = grads(pair_queries, pair_upper, keyed, valued, allowed)
        else:
            pair_upper, pair_queries = upper, queries
        key_total = key_total + jnp.einsum(
            "hqk,qhd->khd", score_grad, pair_queries, preferred_element_type=jnp.float32
        )
        value_total = value_total + jnp.einsum(
            "hqk,qhd->khd", weights, pair_upper, preferred_element_type=jnp.float32
        )
    query_out = (query_grad.reshape(rows, width) * scale).astype(jnp.bfloat16)
    key_out = (key_total.reshape(rows, width) * scale).astype(jnp.bfloat16)
    value_out = value_total.reshape(rows, width).astype(jnp.bfloat16)
    return (query_out, key_out, value_out, gate_grad, w_grad)


def solution(mesh):
    fine = Mesh(
        mesh.devices.reshape(NY, NZ, NX, NC, mesh.devices.shape[1]), BLK + ("grp",)
    )
    every = ("grp",) + BLK
    rows = P(every, None)
    in_specs = (rows, rows, rows, rows, P("grp"), P(BLK, None), rows)
    return jax.shard_map(
        body, mesh=fine, in_specs=in_specs, out_specs=(rows,) * 5, check_vma=False
    )
```

```python
import functools

import jax
import jax.numpy as jnp
import numpy as np
from jax import lax
from jax.experimental import pallas as pl
from jax.experimental.pallas import tpu as pltpu
from jax.sharding import Mesh, PartitionSpec as P

DH = 128
REACH = 4
NY, NZ, NX, NC = 2, 8, 4, 2
COUNT = NY * NZ * NX * NC
BLK = ("y", "z", "x", "c")
ROW = ("x", "c")
COL = ("y", "z")
GROUPS, MEMBERS = NY * NZ, NX * NC
F32, BF16 = jnp.float32, jnp.bfloat16
SCALE = DH ** (-0.5)


def shift(value, steps, sources=None):
    pairs = [(s, s + steps) for s in (sources or range(COUNT)) if 0 <= s + steps < COUNT]
    return lax.ppermute(value, BLK, pairs)


def ring(value, axis, size, steps):
    return lax.ppermute(value, axis, [(s, (s + steps) % size) for s in range(size)])


def swap(value):
    return ring(value, "c", NC, 1)


def dot(a, b, contract):
    return lax.dot_general(a, b, ((contract[:1], contract[1:]), ((), ())), preferred_element_type=F32)


def sigmoid(s):
    return 0.5 * jnp.tanh(0.5 * s) + 0.5


class Loader:
    def __init__(self, sems):
        self.sems, self.used = sems, 0

    def start(self, source, target):
        copy = pltpu.make_async_copy(source, target, self.sems.at[self.used])
        self.used += 1
        copy.start()
        return copy

    def choose(self, condition, source, otherwise, target):
        sem = self.sems.at[self.used]
        self.used += 1

        @pl.when(condition)
        def _():
            pltpu.make_async_copy(source, target, sem).start()

        @pl.when(jnp.logical_not(condition))
        def _():
            pltpu.make_async_copy(otherwise, target, sem).start()

        return pltpu.make_async_copy(source, target, sem)


def allowed_pairs(segs, block, direction):
    rows = segs.shape[1]
    last = segs.shape[0] - 1
    own = jnp.broadcast_to(segs[pl.ds(block, 1), :].astype(F32), (rows, rows)).T
    line = lax.broadcasted_iota(jnp.int32, (rows, rows), 0)
    lane = lax.broadcasted_iota(jnp.int32, (rows, rows), 1)
    masks = []
    for offset in range(REACH):
        there = jnp.clip(block + direction * offset, 0, last)
        mask = own == segs[pl.ds(there, 1), :].astype(F32)
        ahead = direction * (lane - line)
        if offset == 0:
            mask = mask & (ahead >= 0)
        if offset == REACH - 1:
            mask = mask & (ahead <= 0)
        masks.append(mask)
    return jnp.concatenate(masks, 1)


def load_memory(load, even, kv, sib, chip, cross, far, kb, vb):
    rows = kv.shape[0] // 2
    copies = []
    for half, buffer in ((0, kb), (1, vb)):
        part = pl.ds(half * rows, rows)
        slot = lambda o: buffer.at[pl.ds(o * rows, rows), :]
        copies.append(load.start(kv.at[part, :], slot(0)))
        copies.append(load.choose(even, cross.at[part, :], sib.at[part, :], slot(1)))
        copies.append(load.start(chip.at[part, :], slot(2)))
        copies.append(load.choose(even, far.at[part, :], cross.at[part, :], slot(3)))
    return copies


def forward_kernel(
    info, seg, q, kv, sib, chip, cross, far, gate, perm,
    normed_o, rstd_o, hidden_o,
    segs, qb, kb, vb, gb, pb, att, sems,
):
    load = Loader(sems)
    even = info[1] == 0
    first = [load.start(seg, segs), load.start(q, qb)]
    first += load_memory(load, even, kv, sib, chip, cross, far, kb, vb)
    later = [load.start(gate, gb), load.start(perm, pb)]
    for copy in first:
        copy.wait()
    width = qb.shape[1]
    allowed = allowed_pairs(segs, info[0], -1)
    for h in range(width // DH):
        at = pl.ds(h * DH, DH)
        s = dot(qb[:, at], kb[:, at], (1, 1)) * SCALE
        weights = jnp.where(allowed, s * sigmoid(s), 0.0).astype(BF16)
        att[:, at] = dot(weights, vb[:, at], (1, 0))
    attended = att[...]
    mean = jnp.mean(attended, axis=1, keepdims=True)
    centred = attended - mean
    rstd = lax.rsqrt(jnp.mean(centred * centred, axis=1, keepdims=True) + 1e-05)
    normed = centred * rstd
    normed_o[...] = normed
    rstd_o[...] = jnp.broadcast_to(rstd, rstd_o.shape)
    for copy in later:
        copy.wait()
    hidden = (normed * gb[...].astype(F32)).astype(BF16)
    placed = dot(hidden, pb[...], (1, 0)).astype(BF16)
    for k in range(hidden_o.shape[0]):
        hidden_o[k] = placed[:, k * DH:(k + 1) * DH]


def columns_kernel(info, rel, other, w_sub, out):
    rows = out.shape[1]
    for who, block in ((0, rel), (1, other)):
        product = dot(block[...], w_sub[...], (1, 1)).astype(BF16)
        for r in range(NX):
            x = lax.rem(info[2] - r + NX, NX)
            c = info[1] if who == 0 else 1 - info[1]
            out[x * NC + c] = product[r * rows:(r + 1) * rows]


def weight_kernel(info, rel, other, hidden, out):
    total = None
    for who, block in ((0, rel), (1, other)):
        pieces = []
        for r in range(NX):
            x = lax.rem(info[2] - r + NX, NX)
            c = info[1] if who == 0 else 1 - info[1]
            pieces.append(hidden[x * NC + c])
        product = dot(jnp.concatenate(pieces, 0), block[...], (0, 0))
        total = product if total is None else total + product
    out[...] = total


def upstream_kernel(hg, normed, rstd, gate, q, perm, gate_o, uq_o):
    rows = q.shape[0]
    placed = jnp.concatenate([hg[k] for k in range(hg.shape[0])], 1)
    hidden_grad = dot(placed, perm[...], (1, 1))
    n = normed[...]
    gate_o[...] = (hidden_grad * n).astype(BF16)
    normed_grad = hidden_grad * gate[...].astype(F32)
    inner = (
        normed_grad
        - jnp.mean(normed_grad, axis=1, keepdims=True)
        - n * jnp.mean(normed_grad * n, axis=1, keepdims=True)
    )
    uq_o[:rows] = (rstd[:, :1] * inner).astype(BF16)
    uq_o[rows:] = q[...]


def query_kernel(
    info, seg, uq, kv, sib, chip, cross, far,
    query_o,
    segs, ub, kb, vb, sems,
):
    load = Loader(sems)
    even = info[1] == 0
    copies = [load.start(seg, segs), load.start(uq, ub)]
    copies += load_memory(load, even, kv, sib, chip, cross, far, kb, vb)
    for copy in copies:
        copy.wait()
    rows, width = query_o.shape
    allowed = allowed_pairs(segs, info[0], -1)
    for h in range(width // DH):
        at = pl.ds(h * DH, DH)
        keyed = kb[:, at]
        s = dot(ub[rows:, at], keyed, (1, 1)) * SCALE
        sigma = sigmoid(s)
        weight_grad = dot(ub[:rows, at], vb[:, at], (1, 1))
        score_grad = jnp.where(allowed, weight_grad * sigma * (1.0 + s * (1.0 - sigma)), 0.0)
        query_o[:, at] = (dot(score_grad.astype(BF16), keyed, (1, 0)) * SCALE).astype(BF16)


def memory_kernel(
    info, seg, kv, uq, sib, chip, cross, far,
    key_o, value_o,
    segs, kvb, ub, qb, sems,
):
    load = Loader(sems)
    even = info[1] == 0
    rows, width = key_o.shape
    copies = [load.start(seg, segs), load.start(kv, kvb)]
    for half, buffer in ((0, ub), (1, qb)):
        part = pl.ds(half * rows, rows)
        slot = lambda o: buffer.at[pl.ds(o * rows, rows), :]
        copies.append(load.start(uq.at[part, :], slot(0)))
        copies.append(load.choose(even, sib.at[part, :], cross.at[part, :], slot(1)))
        copies.append(load.start(chip.at[part, :], slot(2)))
        copies.append(load.choose(even, cross.at[part, :], far.at[part, :], slot(3)))
    for copy in copies:
        copy.wait()
    allowed = allowed_pairs(segs, info[0], 1)
    for h in range(width // DH):
        at = pl.ds(h * DH, DH)
        queries, upper = qb[:, at], ub[:, at]
        s = dot(kvb[:rows, at], queries, (1, 1)) * SCALE
        sigma = sigmoid(s)
        weights = jnp.where(allowed, s * sigma, 0.0).astype(BF16)
        weight_grad = dot(kvb[rows:, at], upper, (1, 1))
        score_grad = jnp.where(allowed, weight_grad * sigma * (1.0 + s * (1.0 - sigma)), 0.0)
        key_o[:, at] = (dot(score_grad.astype(BF16), queries, (1, 0)) * SCALE).astype(BF16)
        value_o[:, at] = dot(weights, upper, (1, 0)).astype(BF16)


def call(kernel, out_shape, kinds, scratch=(), cost=None):
    place = {"s": pltpu.SMEM, "v": pltpu.VMEM, "a": pl.ANY}
    outs = jax.tree.map(lambda _: pl.BlockSpec(memory_space=pltpu.VMEM), out_shape)
    return pl.pallas_call(
        kernel,
        out_shape=out_shape,
        in_specs=[pl.BlockSpec(memory_space=place[kind]) for kind in kinds],
        out_specs=outs,
        scratch_shapes=list(scratch),
        compiler_params=pltpu.CompilerParams(vmem_limit_bytes=40 * 1024 * 1024),
        cost_estimate=cost,
    )


def body(query_rows, key_rows, value_rows, gate_rows, segment, w_out, cotangent):
    rows, width = query_rows.shape
    device = lax.axis_index(BLK)
    info = jnp.stack([device, lax.axis_index("c"), lax.axis_index("x")]).astype(jnp.int32)
    seg = segment.reshape(-1, rows)
    unit = w_out.shape[0]
    span = REACH * rows

    natural = np.arange(width)
    placed = (natural // unit % MEMBERS) * (GROUPS * unit) + natural // (unit * MEMBERS) * unit + natural % unit
    perm = jnp.asarray(np.eye(width, dtype=np.float32)[:, np.argsort(placed)], BF16)

    def like(*shape, dtype=BF16):
        return jax.ShapeDtypeStruct(shape, dtype)

    def scratch(*shape, dtype=BF16):
        return pltpu.VMEM(shape, dtype)

    def cost(flops, size):
        return pl.CostEstimate(flops=flops, bytes_accessed=size, transcendentals=0)

    seg_scratch = scratch(*seg.shape, dtype=jnp.int32)
    sems = lambda n: pltpu.SemaphoreType.DMA((n,))

    kv = jnp.concatenate([key_rows, value_rows], 0)
    kv_chip = shift(kv, 2)
    kv_far = shift(kv, 3, range(1, COUNT, 2))
    kv_sib = swap(kv)
    kv_cross = swap(kv_chip)
    memory = (kv, kv_sib, kv_chip, kv_cross, kv_far)

    rel = jnp.concatenate([cotangent] + [ring(cotangent, "x", NX, k) for k in range(1, NX)], 0)
    other = swap(rel)
    w_sub = lax.all_to_all(
        jnp.broadcast_to(w_out[None], (GROUPS,) + w_out.shape), COL, 0, 0, tiled=True
    ).reshape(GROUPS * unit, width)
    hg = call(columns_kernel, like(MEMBERS, rows, GROUPS * unit), "svvv", cost=cost(268435456, 2 << 20))(
        info, rel, other, w_sub
    )
    hg = lax.all_to_all(hg, ROW, 0, 0, tiled=True)

    normed, rstd, hidden = call(
        forward_kernel,
        (like(rows, width, dtype=F32), like(rows, 128, dtype=F32), like(MEMBERS, rows, GROUPS * unit)),
        "s" + "a" * 9,
        [
            seg_scratch, scratch(rows, width), scratch(span, width), scratch(span, width),
            scratch(rows, width), scratch(width, width), scratch(rows, width, dtype=F32), sems(12),
        ],
        cost(536870912, 6 << 20),
    )(info, seg, query_rows, *memory, gate_rows, perm)

    hidden_all = lax.all_to_all(hidden, ROW, 0, 0, tiled=True)
    w_part = call(weight_kernel, like(GROUPS * unit, width, dtype=F32), "svvv", cost=cost(268435456, 3 << 20))(
        info, rel, other, hidden_all
    )
    w_parts = lax.all_to_all(w_part.reshape(GROUPS, unit, width), COL, 0, 0, tiled=True)
    w_grad = jnp.sum(w_parts, axis=0)

    gate_grad, uq = call(upstream_kernel, (like(rows, width), like(2 * rows, width)), "vvvvvv", cost=cost(268435456, 4 << 20))(
        hg, normed, rstd, gate_rows, query_rows, perm
    )

    uq_chip = shift(uq, -2)
    uq_far = shift(uq, -3, range(0, COUNT, 2))
    uq_sib = swap(uq)
    uq_cross = swap(uq_chip)

    query_grad = call(
        query_kernel,
        like(rows, width),
        "s" + "a" * 7,
        [seg_scratch, scratch(2 * rows, width), scratch(span, width), scratch(span, width), sems(10)],
        cost(536870912, 5 << 20),
    )(info, seg, uq, *memory)
    key_grad, value_grad = call(
        memory_kernel,
        (like(rows, width), like(rows, width)),
        "s" + "a" * 7,
        [seg_scratch, scratch(2 * rows, width), scratch(span, width), scratch(span, width), sems(10)],
        cost(671088640, 5 << 20),
    )(info, seg, kv, uq, uq_sib, uq_chip, uq_cross, uq_far)
    return (query_grad, key_grad, value_grad, gate_grad, w_grad)


def solution(mesh):
    fine = Mesh(
        mesh.devices.reshape(NY, NZ, NX, NC, mesh.devices.shape[1]), BLK + ("grp",)
    )
    every = ("grp",) + BLK
    rows = P(every, None)
    in_specs = (rows, rows, rows, rows, P("grp"), P(BLK, None), rows)
    return jax.shard_map(
        body, mesh=fine, in_specs=in_specs, out_specs=(rows,) * 5, check_vma=False
    )
```

```python
import jax
import jax.numpy as jnp
import numpy as np
from jax import lax
from jax.experimental import pallas as pl
from jax.experimental.pallas import tpu as pltpu
from jax.sharding import Mesh, PartitionSpec as P

DH = 128
REACH = 4
NY, NZ, NX, NC = 2, 8, 4, 2
COUNT = NY * NZ * NX * NC
BLK = ("y", "z", "x", "c")
PLANE = ("y", "x")
CHIPS = NY * NZ * NX
F32, BF16 = jnp.float32, jnp.bfloat16
SCALE = DH ** (-0.5)
VMEM_LIMIT = 20 * 1024 * 1024


def shift(value, steps, sources=None):
    pairs = [(s, s + steps) for s in (sources or range(COUNT)) if 0 <= s + steps < COUNT]
    return lax.ppermute(value, BLK, pairs)


def ring(value, axis, size, steps):
    return lax.ppermute(value, axis, [(s, (s + steps) % size) for s in range(size)])


def swap(value):
    return ring(value, "c", NC, 1)


def dot(a, b, contract):
    return lax.dot_general(a, b, ((contract[:1], contract[1:]), ((), ())), preferred_element_type=F32)


def sigmoid(s):
    return 0.5 * jnp.tanh(0.5 * s) + 0.5


class Loader:
    def __init__(self, sems):
        self.sems, self.used = sems, 0

    def start(self, source, target):
        copy = pltpu.make_async_copy(source, target, self.sems.at[self.used])
        self.used += 1
        copy.start()
        return copy

    def choose(self, condition, source, otherwise, target):
        sem = self.sems.at[self.used]
        self.used += 1

        @pl.when(condition)
        def _():
            pltpu.make_async_copy(source, target, sem).start()

        @pl.when(jnp.logical_not(condition))
        def _():
            pltpu.make_async_copy(otherwise, target, sem).start()

        return pltpu.make_async_copy(source, target, sem)


def allowed_pairs(segs, block, direction):
    rows = segs.shape[1]
    last = segs.shape[0] - 1
    own = jnp.broadcast_to(segs[pl.ds(block, 1), :].astype(F32), (rows, rows)).T
    line = lax.broadcasted_iota(jnp.int32, (rows, rows), 0)
    lane = lax.broadcasted_iota(jnp.int32, (rows, rows), 1)
    masks = []
    for offset in range(REACH):
        there = jnp.clip(block + direction * offset, 0, last)
        mask = own == segs[pl.ds(there, 1), :].astype(F32)
        ahead = direction * (lane - line)
        if offset == 0:
            mask = mask & (ahead >= 0)
        if offset == REACH - 1:
            mask = mask & (ahead <= 0)
        masks.append(mask)
    return jnp.concatenate(masks, 1)


def load_memory(load, even, kv, k_pair, v_pair, chip, cross, far, kb, vb):
    rows = kv.shape[0] // 2
    copies = []
    for half, pair, buffer in ((0, k_pair, kb), (1, v_pair, vb)):
        part = pl.ds(half * rows, rows)
        slot = lambda o: buffer.at[pl.ds(o * rows, rows), :]
        copies.append(load.start(kv.at[part, :], slot(0)))
        copies.append(load.choose(even, cross.at[part, :], pair.at[pl.ds(0, rows), :], slot(1)))
        copies.append(load.start(chip.at[part, :], slot(2)))
        copies.append(load.choose(even, far.at[part, :], cross.at[part, :], slot(3)))
    return copies


def forward_kernel(
    info, seg, q, kv, k_pair, v_pair, chip, cross, far, gate, perm,
    normed_o, rstd_o, hidden_o,
    segs, qb, kb, vb, gb, pb, att, sems,
):
    load = Loader(sems)
    even = info[1] == 0
    first = [load.start(seg, segs), load.start(q, qb)]
    first += load_memory(load, even, kv, k_pair, v_pair, chip, cross, far, kb, vb)
    later = [load.start(gate, gb), load.start(perm, pb)]
    for copy in first:
        copy.wait()
    width = qb.shape[1]
    allowed = allowed_pairs(segs, info[0], -1)
    for h in range(width // DH):
        at = pl.ds(h * DH, DH)
        s = dot(qb[:, at], kb[:, at], (1, 1)) * SCALE
        weights = jnp.where(allowed, s * sigmoid(s), 0.0).astype(BF16)
        att[:, at] = dot(weights, vb[:, at], (1, 0))
    attended = att[...]
    mean = jnp.mean(attended, axis=1, keepdims=True)
    centred = attended - mean
    rstd = lax.rsqrt(jnp.mean(centred * centred, axis=1, keepdims=True) + 1e-05)
    normed = centred * rstd
    normed_o[...] = normed
    rstd_o[...] = jnp.broadcast_to(rstd, rstd_o.shape)
    for copy in later:
        copy.wait()
    hidden = (normed * gb[...].astype(F32)).astype(BF16)
    hidden_o[...] = dot(hidden, pb[...], (1, 0)).astype(BF16)


def columns_kernel(info, cot, w_sub, mine_o, sent_o, wb, sems):
    load = Loader(sems)
    rows, half = mine_o.shape
    step = half // 4
    chunks = [pl.ds(i * step, step) for i in range(half // step)]
    copies = [load.start(w_sub.at[chunk, :], wb.at[chunk, :]) for chunk in chunks]
    core = info[1]
    own = pl.ds(pl.multiple_of(core * rows, rows), rows)
    other = pl.ds(pl.multiple_of((1 - core) * rows, rows), rows)
    for chunk, copy in zip(chunks, copies):
        copy.wait()
        mine_o[:, chunk] = dot(cot[own, :], wb[chunk, :], (1, 1))
        sent_o[:, chunk] = dot(cot[other, :], wb[chunk, :], (1, 1))


def weight_kernel(info, hidden, cot, out):
    half = out.shape[0]
    columns = hidden[:, pl.ds(pl.multiple_of(info[1] * half, half), half)]
    out[...] = dot(columns, cot[...], (0, 0)).astype(BF16)


def upstream_kernel(info, mine, both, normed, rstd, gate, perm, gate_o, upper_o):
    rows = mine.shape[0]
    own = mine[...]
    even = info[1] == 0
    first = jnp.where(even, own, both[:rows])
    second = jnp.where(even, both[rows:], own)
    placed = jnp.concatenate([first, second], 1)
    high = placed.astype(BF16)
    low = (placed - high.astype(F32)).astype(BF16)
    hidden_grad = dot(high, perm[...], (1, 1)) + dot(low, perm[...], (1, 1))
    n = normed[...]
    gate_o[...] = (hidden_grad * n).astype(BF16)
    normed_grad = hidden_grad * gate[...].astype(F32)
    inner = (
        normed_grad
        - jnp.mean(normed_grad, axis=1, keepdims=True)
        - n * jnp.mean(normed_grad * n, axis=1, keepdims=True)
    )
    upper_o[...] = (rstd[:, :1] * inner).astype(BF16)


def query_kernel(
    info, seg, q, u, kv, k_pair, v_pair, chip, cross, far,
    query_o,
    segs, qb, ub, kb, vb, sems,
):
    load = Loader(sems)
    even = info[1] == 0
    copies = [load.start(seg, segs), load.start(q, qb), load.start(u, ub)]
    copies += load_memory(load, even, kv, k_pair, v_pair, chip, cross, far, kb, vb)
    for copy in copies:
        copy.wait()
    width = query_o.shape[1]
    allowed = allowed_pairs(segs, info[0], -1)
    for h in range(width // DH):
        at = pl.ds(h * DH, DH)
        keyed = kb[:, at]
        s = dot(qb[:, at], keyed, (1, 1)) * SCALE
        sigma = sigmoid(s)
        weight_grad = dot(ub[:, at], vb[:, at], (1, 1))
        score_grad = jnp.where(allowed, weight_grad * sigma * (1.0 + s * (1.0 - sigma)), 0.0)
        query_o[:, at] = (dot(score_grad.astype(BF16), keyed, (1, 0)) * SCALE).astype(BF16)


def memory_kernel(
    info, seg, kv, q, q_pair, q_chip, q_chips, q_far, u, u_pair, u_chip, u_chips, u_far,
    key_o, value_o,
    segs, kvb, qb, ub, sems,
):
    load = Loader(sems)
    even = info[1] == 0
    rows, width = key_o.shape
    copies = [load.start(seg, segs), load.start(kv, kvb)]
    slot = lambda buffer, o: buffer.at[pl.ds(o * rows, rows), :]
    first, second = pl.ds(0, rows), pl.ds(rows, rows)
    for buffer, own, pair, chip, chips, far in (
        (qb, q, q_pair, q_chip, q_chips, q_far),
        (ub, u, u_pair, u_chip, u_chips, u_far),
    ):
        copies.append(load.start(own, slot(buffer, 0)))
        copies.append(load.choose(even, pair.at[second, :], chips.at[first, :], slot(buffer, 1)))
        copies.append(load.start(chip, slot(buffer, 2)))
        copies.append(load.choose(even, chips.at[second, :], far, slot(buffer, 3)))
    for copy in copies:
        copy.wait()
    allowed = allowed_pairs(segs, info[0], 1)
    for h in range(width // DH):
        at = pl.ds(h * DH, DH)
        queries, upper = qb[:, at], ub[:, at]
        s = dot(kvb[:rows, at], queries, (1, 1)) * SCALE
        sigma = sigmoid(s)
        weights = jnp.where(allowed, s * sigma, 0.0).astype(BF16)
        weight_grad = dot(kvb[rows:, at], upper, (1, 1))
        score_grad = jnp.where(allowed, weight_grad * sigma * (1.0 + s * (1.0 - sigma)), 0.0)
        key_o[:, at] = (dot(score_grad.astype(BF16), queries, (1, 0)) * SCALE).astype(BF16)
        value_o[:, at] = dot(weights, upper, (1, 0)).astype(BF16)


def sum_kernel(parts, out):
    total = parts[0].astype(F32)
    for i in range(1, parts.shape[0]):
        total += parts[i].astype(F32)
    out[...] = total


def pack_kernel(key, value, out, sems):
    load = Loader(sems)
    rows = key.shape[0]
    copies = [load.start(key, out.at[pl.ds(0, rows), :]), load.start(value, out.at[pl.ds(rows, rows), :])]
    for copy in copies:
        copy.wait()


def call(kernel, out_shape, kinds, scratch=(), work=1000):
    place = {"s": pltpu.SMEM, "v": pltpu.VMEM, "a": pl.ANY, "h": pltpu.HBM}
    return pl.pallas_call(
        kernel,
        out_shape=out_shape,
        in_specs=[pl.BlockSpec(memory_space=place[kind]) for kind in kinds],
        out_specs=jax.tree.map(lambda _: pl.BlockSpec(memory_space=pltpu.VMEM), out_shape),
        scratch_shapes=list(scratch),
        compiler_params=pltpu.CompilerParams(vmem_limit_bytes=VMEM_LIMIT),
        cost_estimate=pl.CostEstimate(flops=work, bytes_accessed=1000, transcendentals=0),
    )


def body(query_rows, key_rows, value_rows, gate_rows, segment, w_out, cotangent):
    rows, width = query_rows.shape
    device = lax.axis_index(BLK)
    info = jnp.stack([device, lax.axis_index("c"), lax.axis_index("x")]).astype(jnp.int32)
    seg = segment.reshape(-1, rows)
    unit = w_out.shape[0]
    span = REACH * rows

    natural = np.arange(width)
    holder = natural // unit
    core, x, z, y = holder % NC, holder // NC % NX, holder // (NC * NX) % NZ, holder // (NC * NX * NZ)
    placed = (((core * NY + y) * NX + x) * NZ + z) * unit + natural % unit
    perm = jnp.asarray(np.eye(width, dtype=np.float32)[:, np.argsort(placed)], BF16)

    def like(*shape, dtype=BF16):
        return jax.ShapeDtypeStruct(shape, dtype)

    def scratch(*shape, dtype=BF16):
        return pltpu.VMEM(shape, dtype)

    seg_scratch = scratch(*seg.shape, dtype=jnp.int32)
    sems = lambda n: pltpu.SemaphoreType.DMA((n,))

    def pair(rows_of):
        return lax.all_gather(rows_of, "c", axis=0, tiled=True)

    def ahead(rows_of):
        return shift(rows_of, -2), shift(rows_of, -3, range(0, COUNT, 2))

    kv = call(pack_kernel, like(2 * rows, width), "hh", [sems(2)])(key_rows, value_rows)
    w_line = lax.all_to_all(
        jnp.broadcast_to(w_out[None], (NZ,) + w_out.shape), "z", 0, 0, tiled=True
    ).reshape(NZ * unit, width)
    kv_chip = shift(kv, 2)
    cot, k_pair, v_pair = pair(cotangent), pair(key_rows), pair(value_rows)
    kv_far = shift(kv, 3, range(1, COUNT, 2))
    q_chip, q_far = ahead(query_rows)
    kv_chip, kv_far, w_line, cot, k_pair, v_pair, q_chip, q_far = lax.optimization_barrier(
        (kv_chip, kv_far, w_line, cot, k_pair, v_pair, q_chip, q_far)
    )
    w_sub = lax.all_to_all(
        jnp.broadcast_to(w_line[None], (NY * NX,) + w_line.shape), PLANE, 0, 0, tiled=True
    ).reshape(CHIPS * unit, width)
    kv_cross = swap(kv_chip)
    memory = (kv, k_pair, v_pair, kv_chip, kv_cross, kv_far)

    normed, rstd, hidden = call(
        forward_kernel,
        (like(rows, width, dtype=F32), like(rows, 128, dtype=F32), like(rows, width)),
        "shhahhhhhhh",
        [
            seg_scratch, scratch(rows, width), scratch(span, width), scratch(span, width),
            scratch(rows, width), scratch(width, width), scratch(rows, width, dtype=F32), sems(12),
        ],
    )(info, seg, query_rows, *memory, gate_rows, perm)
    mine, sent = call(
        columns_kernel,
        (like(rows, CHIPS * unit, dtype=F32),) * 2,
        "svh",
        [scratch(CHIPS * unit, width), sems(4)],
    )(info, cot, w_sub)
    gate_grad, upper = call(upstream_kernel, (like(rows, width), like(rows, width)), "svvvvvv")(
        info, mine, pair(sent), normed, rstd, gate_rows, perm
    )

    u_chip, u_far = ahead(upper)
    u_pair = pair(upper)

    hidden, q_chip, q_far = lax.optimization_barrier((hidden, q_chip, q_far))
    q_pair, q_chips = pair(query_rows), pair(q_chip)
    w_part = call(weight_kernel, like(CHIPS * unit, width), "svv")(info, pair(hidden), cot)
    w_parts = lax.all_to_all(w_part.reshape(NY * NX, NZ * unit, width), PLANE, 0, 0, tiled=True)
    w_parts, _ = lax.optimization_barrier((w_parts, u_pair))
    w_sum = call(sum_kernel, like(NZ * unit, width, dtype=F32), "v")(w_parts).reshape(NZ, unit, width)
    w_line = lax.all_to_all(w_sum, "z", 0, 0, tiled=True)
    upper_late, _ = lax.optimization_barrier((upper, w_sum))
    query_grad = call(
        query_kernel,
        like(rows, width),
        "s" + "a" * 9,
        [
            seg_scratch, scratch(rows, width), scratch(rows, width), scratch(span, width), scratch(span, width),
            sems(11),
        ],
        20_000_000_000,
    )(info, seg, query_rows, upper_late, *memory)
    u_chip, _ = lax.optimization_barrier((u_chip, query_grad))
    u_chips = pair(u_chip)
    key_grad, value_grad = call(
        memory_kernel,
        (like(rows, width), like(rows, width)),
        "s" + "a" * 12,
        [seg_scratch, scratch(2 * rows, width), scratch(span, width), scratch(span, width), sems(10)],
        20_000_000_000,
    )(
        info, seg, kv, query_rows, q_pair, q_chip, q_chips, q_far,
        upper, u_pair, u_chip, u_chips, u_far,
    )
    w_line, _ = lax.optimization_barrier((w_line, key_grad))
    w_grad = call(sum_kernel, like(unit, width, dtype=F32), "v")(w_line)
    return (query_grad, key_grad, value_grad, gate_grad, w_grad)


def solution(mesh):
    fine = Mesh(
        mesh.devices.reshape(NY, NZ, NX, NC, mesh.devices.shape[1]), BLK + ("grp",)
    )
    every = ("grp",) + BLK
    rows = P(every, None)
    in_specs = (rows, rows, rows, rows, P("grp"), P(BLK, None), rows)
    return jax.shard_map(
        body, mesh=fine, in_specs=in_specs, out_specs=(rows,) * 5, check_vma=False
    )
```

```python
import jax
import jax.numpy as jnp
import numpy as np
from jax import lax
from jax.experimental import pallas as pl
from jax.experimental.pallas import tpu as pltpu
from jax.sharding import Mesh, PartitionSpec as P

DH = 128
REACH = 4
NY, NZ, NX, NC = 2, 8, 4, 2
COUNT = NY * NZ * NX * NC
BLK = ("y", "z", "x", "c")
PLANE = ("y", "x")
CHIPS = NY * NZ * NX
F32, BF16 = jnp.float32, jnp.bfloat16
SCALE = DH ** (-0.5)
VMEM_LIMIT = 20 * 1024 * 1024
LARGE_LIMIT = 58 * 1024 * 1024
HEADS_TOGETHER = 2


def shift(value, steps, sources=None):
    pairs = [(s, s + steps) for s in (sources or range(COUNT)) if 0 <= s + steps < COUNT]
    return lax.ppermute(value, BLK, pairs)


def ring(value, axis, size, steps):
    return lax.ppermute(value, axis, [(s, (s + steps) % size) for s in range(size)])


def swap(value):
    return ring(value, "c", NC, 1)


def dot(a, b, contract):
    return lax.dot_general(a, b, ((contract[:1], contract[1:]), ((), ())), preferred_element_type=F32)


def sigmoid(s):
    return 0.5 * jnp.tanh(0.5 * s) + 0.5


class Loader:
    def __init__(self, sems):
        self.sems, self.used = sems, 0

    def start(self, source, target):
        copy = pltpu.make_async_copy(source, target, self.sems.at[self.used])
        self.used += 1
        copy.start()
        return copy

    def choose(self, condition, source, otherwise, target):
        sem = self.sems.at[self.used]
        self.used += 1

        @pl.when(condition)
        def _():
            pltpu.make_async_copy(source, target, sem).start()

        @pl.when(jnp.logical_not(condition))
        def _():
            pltpu.make_async_copy(otherwise, target, sem).start()

        return pltpu.make_async_copy(source, target, sem)


def allowed_pairs(segs, block, direction):
    rows = segs.shape[1]
    last = segs.shape[0] - 1
    own = jnp.broadcast_to(segs[pl.ds(block, 1), :].astype(F32), (rows, rows)).T
    line = lax.broadcasted_iota(jnp.int32, (rows, rows), 0)
    lane = lax.broadcasted_iota(jnp.int32, (rows, rows), 1)
    masks = []
    for offset in range(REACH):
        there = jnp.clip(block + direction * offset, 0, last)
        mask = own == segs[pl.ds(there, 1), :].astype(F32)
        ahead = direction * (lane - line)
        if offset == 0:
            mask = mask & (ahead >= 0)
        if offset == REACH - 1:
            mask = mask & (ahead <= 0)
        masks.append(mask)
    return jnp.concatenate(masks, 1)


def head_groups(width):
    heads = [pl.ds(h * DH, DH) for h in range(width // DH)]
    return [heads[i:i + HEADS_TOGETHER] for i in range(0, len(heads), HEADS_TOGETHER)]


def load_memory(load, even, kv, k_pair, v_pair, chip, cross, far, kb, vb):
    rows = kv.shape[0] // 2
    copies = []
    for half, pair, buffer in ((0, k_pair, kb), (1, v_pair, vb)):
        part = pl.ds(half * rows, rows)
        slot = lambda o: buffer.at[pl.ds(o * rows, rows), :]
        copies.append(load.start(kv.at[part, :], slot(0)))
        copies.append(load.choose(even, cross.at[part, :], pair.at[pl.ds(0, rows), :], slot(1)))
        copies.append(load.start(chip.at[part, :], slot(2)))
        copies.append(load.choose(even, far.at[part, :], cross.at[part, :], slot(3)))
    return copies


def forward_kernel(
    info, seg, q, kv, k_pair, v_pair, chip, cross, far, gate, perm,
    normed_o, rstd_o, hidden_o,
    segs, qb, kb, vb, gb, pb, att, sems,
):
    load = Loader(sems)
    even = info[1] == 0
    first = [load.start(seg, segs), load.start(q, qb)]
    first += load_memory(load, even, kv, k_pair, v_pair, chip, cross, far, kb, vb)
    later = [load.start(gate, gb), load.start(perm, pb)]
    for copy in first:
        copy.wait()
    width = qb.shape[1]
    allowed = allowed_pairs(segs, info[0], -1)
    for at in head_groups(width):
        scores = [dot(qb[:, h], kb[:, h], (1, 1)) * SCALE for h in at]
        weights = [jnp.where(allowed, s * sigmoid(s), 0.0).astype(BF16) for s in scores]
        for h, w in zip(at, weights):
            att[:, h] = dot(w, vb[:, h], (1, 0))
    attended = att[...]
    mean = jnp.mean(attended, axis=1, keepdims=True)
    centred = attended - mean
    rstd = lax.rsqrt(jnp.mean(centred * centred, axis=1, keepdims=True) + 1e-05)
    normed = centred * rstd
    normed_o[...] = normed
    rstd_o[...] = jnp.broadcast_to(rstd, rstd_o.shape)
    for copy in later:
        copy.wait()
    hidden = (normed * gb[...].astype(F32)).astype(BF16)
    hidden_o[...] = dot(hidden, pb[...], (1, 0)).astype(BF16)


def columns_kernel(info, cot, w_sub, mine_o, sent_o, wb, sems):
    load = Loader(sems)
    rows, half = mine_o.shape
    step = half // 4
    chunks = [pl.ds(i * step, step) for i in range(half // step)]
    copies = [load.start(w_sub.at[chunk, :], wb.at[chunk, :]) for chunk in chunks]
    core = info[1]
    own = pl.ds(pl.multiple_of(core * rows, rows), rows)
    other = pl.ds(pl.multiple_of((1 - core) * rows, rows), rows)
    for chunk, copy in zip(chunks, copies):
        copy.wait()
        mine_o[:, chunk] = dot(cot[own, :], wb[chunk, :], (1, 1))
        sent_o[:, chunk] = dot(cot[other, :], wb[chunk, :], (1, 1))


def weight_kernel(info, hidden, cot, out):
    half = out.shape[0]
    columns = hidden[:, pl.ds(pl.multiple_of(info[1] * half, half), half)]
    out[...] = dot(columns, cot[...], (0, 0)).astype(BF16)


def upstream_kernel(info, mine, both, normed, rstd, gate, perm, gate_o, upper_o):
    rows = mine.shape[0]
    own = mine[...]
    even = info[1] == 0
    first = jnp.where(even, own, both[:rows])
    second = jnp.where(even, both[rows:], own)
    placed = jnp.concatenate([first, second], 1)
    high = placed.astype(BF16)
    low = (placed - high.astype(F32)).astype(BF16)
    hidden_grad = dot(high, perm[...], (1, 1)) + dot(low, perm[...], (1, 1))
    n = normed[...]
    gate_o[...] = (hidden_grad * n).astype(BF16)
    normed_grad = hidden_grad * gate[...].astype(F32)
    inner = (
        normed_grad
        - jnp.mean(normed_grad, axis=1, keepdims=True)
        - n * jnp.mean(normed_grad * n, axis=1, keepdims=True)
    )
    upper_o[...] = (rstd[:, :1] * inner).astype(BF16)


def query_kernel(
    info, seg, q, u, kv, k_pair, v_pair, chip, cross, far,
    query_o,
    segs, qb, ub, kb, vb, sems,
):
    load = Loader(sems)
    even = info[1] == 0
    copies = [load.start(seg, segs), load.start(q, qb), load.start(u, ub)]
    copies += load_memory(load, even, kv, k_pair, v_pair, chip, cross, far, kb, vb)
    for copy in copies:
        copy.wait()
    width = query_o.shape[1]
    allowed = allowed_pairs(segs, info[0], -1)
    for at in head_groups(width):
        scores = [dot(qb[:, h], kb[:, h], (1, 1)) * SCALE for h in at]
        weight_grads = [dot(ub[:, h], vb[:, h], (1, 1)) for h in at]
        score_grads = []
        for s, weight_grad in zip(scores, weight_grads):
            sigma = sigmoid(s)
            grad = jnp.where(allowed, weight_grad * (sigma * (1.0 + s * (1.0 - sigma))), 0.0)
            score_grads.append(grad.astype(BF16))
        for h, grad in zip(at, score_grads):
            query_o[:, h] = (dot(grad, kb[:, h], (1, 0)) * SCALE).astype(BF16)


def memory_kernel(
    info, seg, kv, q, q_pair, q_chip, q_chips, q_far, u, u_pair, u_chip, u_chips, u_far,
    key_o, value_o,
    segs, kvb, qb, ub, sems,
):
    load = Loader(sems)
    even = info[1] == 0
    rows, width = key_o.shape
    copies = [load.start(seg, segs), load.start(kv, kvb)]
    slot = lambda buffer, o: buffer.at[pl.ds(o * rows, rows), :]
    first, second = pl.ds(0, rows), pl.ds(rows, rows)
    for buffer, own, pair, chip, chips, far in (
        (qb, q, q_pair, q_chip, q_chips, q_far),
        (ub, u, u_pair, u_chip, u_chips, u_far),
    ):
        copies.append(load.start(own, slot(buffer, 0)))
        copies.append(load.choose(even, pair.at[second, :], chips.at[first, :], slot(buffer, 1)))
        copies.append(load.start(chip, slot(buffer, 2)))
        copies.append(load.choose(even, chips.at[second, :], far, slot(buffer, 3)))
    for copy in copies:
        copy.wait()
    allowed = allowed_pairs(segs, info[0], 1)
    for at in head_groups(width):
        scores = [dot(kvb[:rows, h], qb[:, h], (1, 1)) * SCALE for h in at]
        weight_grads = [dot(kvb[rows:, h], ub[:, h], (1, 1)) for h in at]
        weights, score_grads = [], []
        for s, weight_grad in zip(scores, weight_grads):
            sigma = sigmoid(s)
            weights.append(jnp.where(allowed, s * sigma, 0.0).astype(BF16))
            grad = jnp.where(allowed, weight_grad * (sigma * (1.0 + s * (1.0 - sigma))), 0.0)
            score_grads.append(grad.astype(BF16))
        for h, w, grad in zip(at, weights, score_grads):
            key_o[:, h] = (dot(grad, qb[:, h], (1, 0)) * SCALE).astype(BF16)
            value_o[:, h] = dot(w, ub[:, h], (1, 0)).astype(BF16)


def sum_kernel(parts, out):
    total = parts[0].astype(F32)
    for i in range(1, parts.shape[0]):
        total += parts[i].astype(F32)
    out[...] = total


def pack_kernel(key, value, out, sems):
    load = Loader(sems)
    rows = key.shape[0]
    copies = [load.start(key, out.at[pl.ds(0, rows), :]), load.start(value, out.at[pl.ds(rows, rows), :])]
    for copy in copies:
        copy.wait()


def call(kernel, out_shape, kinds, scratch=(), work=1000, limit=VMEM_LIMIT):
    place = {"s": pltpu.SMEM, "v": pltpu.VMEM, "a": pl.ANY, "h": pltpu.HBM}
    return pl.pallas_call(
        kernel,
        out_shape=out_shape,
        in_specs=[pl.BlockSpec(memory_space=place[kind]) for kind in kinds],
        out_specs=jax.tree.map(lambda _: pl.BlockSpec(memory_space=pltpu.VMEM), out_shape),
        scratch_shapes=list(scratch),
        compiler_params=pltpu.CompilerParams(vmem_limit_bytes=limit),
        cost_estimate=pl.CostEstimate(flops=work, bytes_accessed=1000, transcendentals=0),
    )


def body(query_rows, key_rows, value_rows, gate_rows, segment, w_out, cotangent):
    rows, width = query_rows.shape
    device = lax.axis_index(BLK)
    info = jnp.stack([device, lax.axis_index("c"), lax.axis_index("x")]).astype(jnp.int32)
    seg = segment.reshape(-1, rows)
    unit = w_out.shape[0]
    span = REACH * rows

    natural = np.arange(width)
    holder = natural // unit
    core, x, z, y = holder % NC, holder // NC % NX, holder // (NC * NX) % NZ, holder // (NC * NX * NZ)
    placed = (((core * NY + y) * NX + x) * NZ + z) * unit + natural % unit
    perm = jnp.asarray(np.eye(width, dtype=np.float32)[:, np.argsort(placed)], BF16)

    def like(*shape, dtype=BF16):
        return jax.ShapeDtypeStruct(shape, dtype)

    def scratch(*shape, dtype=BF16):
        return pltpu.VMEM(shape, dtype)

    seg_scratch = scratch(*seg.shape, dtype=jnp.int32)
    sems = lambda n: pltpu.SemaphoreType.DMA((n,))

    def pair(rows_of):
        return lax.all_gather(rows_of, "c", axis=0, tiled=True)

    def ahead(rows_of):
        return shift(rows_of, -2), shift(rows_of, -3, range(0, COUNT, 2))

    kv = call(pack_kernel, like(2 * rows, width), "hh", [sems(2)])(key_rows, value_rows)
    w_line = lax.all_to_all(
        jnp.broadcast_to(w_out[None], (NZ,) + w_out.shape), "z", 0, 0, tiled=True
    ).reshape(NZ * unit, width)
    kv_chip = shift(kv, 2)
    cot, k_pair, v_pair = pair(cotangent), pair(key_rows), pair(value_rows)
    kv_far = shift(kv, 3, range(1, COUNT, 2))
    q_chip, q_far = ahead(query_rows)
    kv_chip, kv_far, w_line, cot, k_pair, v_pair, q_chip, q_far = lax.optimization_barrier(
        (kv_chip, kv_far, w_line, cot, k_pair, v_pair, q_chip, q_far)
    )
    w_sub = lax.all_to_all(
        jnp.broadcast_to(w_line[None], (NY * NX,) + w_line.shape), PLANE, 0, 0, tiled=True
    ).reshape(CHIPS * unit, width)
    kv_cross = swap(kv_chip)
    memory = (kv, k_pair, v_pair, kv_chip, kv_cross, kv_far)

    normed, rstd, hidden = call(
        forward_kernel,
        (like(rows, width, dtype=F32), like(rows, 128, dtype=F32), like(rows, width)),
        "shhahhhhhhh",
        [
            seg_scratch, scratch(rows, width), scratch(span, width), scratch(span, width),
            scratch(rows, width), scratch(width, width), scratch(rows, width, dtype=F32), sems(12),
        ],
        limit=LARGE_LIMIT,
    )(info, seg, query_rows, *memory, gate_rows, perm)
    mine, sent = call(
        columns_kernel,
        (like(rows, CHIPS * unit, dtype=F32),) * 2,
        "svh",
        [scratch(CHIPS * unit, width), sems(4)],
    )(info, cot, w_sub)
    gate_grad, upper = call(upstream_kernel, (like(rows, width), like(rows, width)), "svvvvvv")(
        info, mine, pair(sent), normed, rstd, gate_rows, perm
    )

    u_chip, u_far = ahead(upper)
    u_pair = pair(upper)

    hidden, q_chip, q_far = lax.optimization_barrier((hidden, q_chip, q_far))
    w_part = call(weight_kernel, like(CHIPS * unit, width), "svv")(info, pair(hidden), cot)
    w_parts = lax.all_to_all(w_part.reshape(NY * NX, NZ * unit, width), PLANE, 0, 0, tiled=True)
    q_late, q_chip_late, _ = lax.optimization_barrier((query_rows, q_chip, u_pair))
    q_pair, q_chips = pair(q_late), pair(q_chip_late)
    w_parts, _ = lax.optimization_barrier((w_parts, u_pair))
    w_sum = call(sum_kernel, like(NZ * unit, width, dtype=F32), "v")(w_parts).reshape(NZ, unit, width)
    w_line = lax.all_to_all(w_sum, "z", 0, 0, tiled=True)
    upper_late, _ = lax.optimization_barrier((upper, w_sum))
    query_grad = call(
        query_kernel,
        like(rows, width),
        "s" + "a" * 9,
        [
            seg_scratch, scratch(rows, width), scratch(rows, width), scratch(span, width), scratch(span, width),
            sems(11),
        ],
        20_000_000_000,
        LARGE_LIMIT,
    )(info, seg, query_rows, upper_late, *memory)
    u_chip, _ = lax.optimization_barrier((u_chip, query_grad))
    u_chips = pair(u_chip)
    key_grad, value_grad = call(
        memory_kernel,
        (like(rows, width), like(rows, width)),
        "s" + "a" * 12,
        [seg_scratch, scratch(2 * rows, width), scratch(span, width), scratch(span, width), sems(10)],
        20_000_000_000,
    )(
        info, seg, kv, query_rows, q_pair, q_chip, q_chips, q_far,
        upper, u_pair, u_chip, u_chips, u_far,
    )
    w_line, _ = lax.optimization_barrier((w_line, key_grad))
    w_grad = call(sum_kernel, like(unit, width, dtype=F32), "v")(w_line)
    return (query_grad, key_grad, value_grad, gate_grad, w_grad)


def solution(mesh):
    fine = Mesh(
        mesh.devices.reshape(NY, NZ, NX, NC, mesh.devices.shape[1]), BLK + ("grp",)
    )
    every = ("grp",) + BLK
    rows = P(every, None)
    in_specs = (rows, rows, rows, rows, P("grp"), P(BLK, None), rows)
    return jax.shard_map(
        body, mesh=fine, in_specs=in_specs, out_specs=(rows,) * 5, check_vma=False
    )
```

```python
import jax
import jax.numpy as jnp
import numpy as np
from jax import lax
from jax.experimental import pallas as pl
from jax.experimental.pallas import tpu as pltpu
from jax.sharding import Mesh, PartitionSpec as P

DH = 128
REACH = 4
NY, NZ, NX, NC = 2, 8, 4, 2
COUNT = NY * NZ * NX * NC
BLK = ("y", "z", "x", "c")
PLANE = ("y", "x")
CHIPS = NY * NZ * NX
F32, BF16 = jnp.float32, jnp.bfloat16
SCALE = DH ** (-0.5)
VMEM_LIMIT = 20 * 1024 * 1024
LARGE_LIMIT = 58 * 1024 * 1024
HEADS_TOGETHER = 2


def shift(value, steps, sources=None):
    pairs = [(s, s + steps) for s in (sources or range(COUNT)) if 0 <= s + steps < COUNT]
    return lax.ppermute(value, BLK, pairs)


def ring(value, axis, size, steps):
    return lax.ppermute(value, axis, [(s, (s + steps) % size) for s in range(size)])


def swap(value):
    return ring(value, "c", NC, 1)


def dot(a, b, contract):
    return lax.dot_general(a, b, ((contract[:1], contract[1:]), ((), ())), preferred_element_type=F32)


def sigmoid(s):
    return 0.5 * jnp.tanh(0.5 * s) + 0.5


def position():
    y, z, x, c = (lax.axis_index(axis) for axis in BLK)
    return ((y * NZ + z) * NX + x) * NC + c, c


class Loader:
    def __init__(self, sems):
        self.sems, self.used = sems, 0

    def start(self, source, target):
        copy = pltpu.make_async_copy(source, target, self.sems.at[self.used])
        self.used += 1
        copy.start()
        return copy

    def choose(self, condition, source, otherwise, target):
        sem = self.sems.at[self.used]
        self.used += 1

        @pl.when(condition)
        def _():
            pltpu.make_async_copy(source, target, sem).start()

        @pl.when(jnp.logical_not(condition))
        def _():
            pltpu.make_async_copy(otherwise, target, sem).start()

        return pltpu.make_async_copy(source, target, sem)


def allowed_pairs(segs, block, direction):
    rows = segs.shape[1]
    last = segs.shape[0] - 1
    own = jnp.broadcast_to(segs[pl.ds(block, 1), :].astype(F32), (rows, rows)).T
    line = lax.broadcasted_iota(jnp.int32, (rows, rows), 0)
    lane = lax.broadcasted_iota(jnp.int32, (rows, rows), 1)
    masks = []
    for offset in range(REACH):
        there = jnp.clip(block + direction * offset, 0, last)
        mask = own == segs[pl.ds(there, 1), :].astype(F32)
        ahead = direction * (lane - line)
        if offset == 0:
            mask = mask & (ahead >= 0)
        if offset == REACH - 1:
            mask = mask & (ahead <= 0)
        masks.append(mask)
    return jnp.concatenate(masks, 1)


def head_groups(width):
    heads = [pl.ds(h * DH, DH) for h in range(width // DH)]
    return [heads[i:i + HEADS_TOGETHER] for i in range(0, len(heads), HEADS_TOGETHER)]


def load_memory(load, even, kv, k_pair, v_pair, chip, cross, far, kb, vb):
    rows = kv.shape[0] // 2
    copies = []
    for half, pair, buffer in ((0, k_pair, kb), (1, v_pair, vb)):
        part = pl.ds(half * rows, rows)
        slot = lambda o: buffer.at[pl.ds(o * rows, rows), :]
        copies.append(load.start(kv.at[part, :], slot(0)))
        copies.append(load.choose(even, cross.at[part, :], pair.at[pl.ds(0, rows), :], slot(1)))
        copies.append(load.start(chip.at[part, :], slot(2)))
        copies.append(load.choose(even, far.at[part, :], cross.at[part, :], slot(3)))
    return copies


def forward_kernel(
    seg, q, kv, k_pair, v_pair, chip, cross, far, gate, perm,
    normed_o, rstd_o, hidden_o,
    segs, qb, kb, vb, gb, pb, att, sems,
):
    load = Loader(sems)
    block, core = position()
    even = core == 0
    first = [load.start(seg, segs), load.start(q, qb)]
    first += load_memory(load, even, kv, k_pair, v_pair, chip, cross, far, kb, vb)
    later = [load.start(gate, gb), load.start(perm, pb)]
    for copy in first:
        copy.wait()
    width = qb.shape[1]
    allowed = allowed_pairs(segs, block, -1)
    for at in head_groups(width):
        scores = [dot(qb[:, h], kb[:, h], (1, 1)) * SCALE for h in at]
        weights = [jnp.where(allowed, s * sigmoid(s), 0.0).astype(BF16) for s in scores]
        for h, w in zip(at, weights):
            att[:, h] = dot(w, vb[:, h], (1, 0))
    attended = att[...]
    mean = jnp.mean(attended, axis=1, keepdims=True)
    centred = attended - mean
    rstd = lax.rsqrt(jnp.mean(centred * centred, axis=1, keepdims=True) + 1e-05)
    normed = centred * rstd
    normed_o[...] = normed
    rstd_o[...] = jnp.broadcast_to(rstd, rstd_o.shape)
    for copy in later:
        copy.wait()
    hidden = (normed * gb[...].astype(F32)).astype(BF16)
    hidden_o[...] = dot(hidden, pb[...], (1, 0)).astype(BF16)


def columns_kernel(cot, w_sub, mine_o, sent_o, wb, sems):
    load = Loader(sems)
    rows, half = mine_o.shape
    step = half // 4
    chunks = [pl.ds(i * step, step) for i in range(half // step)]
    copies = [load.start(w_sub.at[chunk, :], wb.at[chunk, :]) for chunk in chunks]
    core = position()[1]
    own = pl.ds(pl.multiple_of(core * rows, rows), rows)
    other = pl.ds(pl.multiple_of((1 - core) * rows, rows), rows)
    for chunk, copy in zip(chunks, copies):
        copy.wait()
        mine_o[:, chunk] = dot(cot[own, :], wb[chunk, :], (1, 1))
        sent_o[:, chunk] = dot(cot[other, :], wb[chunk, :], (1, 1))


def weight_kernel(hidden, cot, out):
    half = out.shape[0]
    columns = hidden[:, pl.ds(pl.multiple_of(position()[1] * half, half), half)]
    out[...] = dot(columns, cot[...], (0, 0)).astype(BF16)


def upstream_kernel(mine, both, normed, rstd, gate, perm, gate_o, upper_o):
    rows = mine.shape[0]
    own = mine[...]
    block, core = position()
    even = core == 0
    first = jnp.where(even, own, both[:rows])
    second = jnp.where(even, both[rows:], own)
    placed = jnp.concatenate([first, second], 1)
    high = placed.astype(BF16)
    low = (placed - high.astype(F32)).astype(BF16)
    hidden_grad = dot(high, perm[...], (1, 1)) + dot(low, perm[...], (1, 1))
    n = normed[...]
    gate_o[...] = (hidden_grad * n).astype(BF16)
    normed_grad = hidden_grad * gate[...].astype(F32)
    inner = (
        normed_grad
        - jnp.mean(normed_grad, axis=1, keepdims=True)
        - n * jnp.mean(normed_grad * n, axis=1, keepdims=True)
    )
    upper_o[...] = (rstd[:, :1] * inner).astype(BF16)


def query_kernel(
    seg, q, u, kv, k_pair, v_pair, chip, cross, far,
    query_o,
    segs, qb, ub, kb, vb, sems,
):
    load = Loader(sems)
    block, core = position()
    even = core == 0
    copies = [load.start(seg, segs), load.start(q, qb), load.start(u, ub)]
    copies += load_memory(load, even, kv, k_pair, v_pair, chip, cross, far, kb, vb)
    for copy in copies:
        copy.wait()
    width = query_o.shape[1]
    allowed = allowed_pairs(segs, block, -1)
    for at in head_groups(width):
        scores = [dot(qb[:, h], kb[:, h], (1, 1)) * SCALE for h in at]
        weight_grads = [dot(ub[:, h], vb[:, h], (1, 1)) for h in at]
        score_grads = []
        for s, weight_grad in zip(scores, weight_grads):
            sigma = sigmoid(s)
            grad = jnp.where(allowed, weight_grad * (sigma * (1.0 + s * (1.0 - sigma))), 0.0)
            score_grads.append(grad.astype(BF16))
        for h, grad in zip(at, score_grads):
            query_o[:, h] = (dot(grad, kb[:, h], (1, 0)) * SCALE).astype(BF16)


def memory_kernel(
    seg, kv, q, q_pair, q_chip, q_chips, q_far, u, u_pair, u_chip, u_chips, u_far,
    key_o, value_o,
    segs, kvb, qb, ub, sems,
):
    load = Loader(sems)
    block, core = position()
    even = core == 0
    rows, width = key_o.shape
    copies = [load.start(seg, segs), load.start(kv, kvb)]
    slot = lambda buffer, o: buffer.at[pl.ds(o * rows, rows), :]
    first, second = pl.ds(0, rows), pl.ds(rows, rows)
    for buffer, own, pair, chip, chips, far in (
        (qb, q, q_pair, q_chip, q_chips, q_far),
        (ub, u, u_pair, u_chip, u_chips, u_far),
    ):
        copies.append(load.start(own, slot(buffer, 0)))
        copies.append(load.choose(even, pair.at[second, :], chips.at[first, :], slot(buffer, 1)))
        copies.append(load.start(chip, slot(buffer, 2)))
        copies.append(load.choose(even, chips.at[second, :], far, slot(buffer, 3)))
    for copy in copies:
        copy.wait()
    allowed = allowed_pairs(segs, block, 1)
    for at in head_groups(width):
        scores = [dot(kvb[:rows, h], qb[:, h], (1, 1)) * SCALE for h in at]
        weight_grads = [dot(kvb[rows:, h], ub[:, h], (1, 1)) for h in at]
        weights, score_grads = [], []
        for s, weight_grad in zip(scores, weight_grads):
            sigma = sigmoid(s)
            weights.append(jnp.where(allowed, s * sigma, 0.0).astype(BF16))
            grad = jnp.where(allowed, weight_grad * (sigma * (1.0 + s * (1.0 - sigma))), 0.0)
            score_grads.append(grad.astype(BF16))
        for h, w, grad in zip(at, weights, score_grads):
            key_o[:, h] = (dot(grad, qb[:, h], (1, 0)) * SCALE).astype(BF16)
            value_o[:, h] = dot(w, ub[:, h], (1, 0)).astype(BF16)


def sum_kernel(parts, out):
    total = parts[0].astype(F32)
    for i in range(1, parts.shape[0]):
        total += parts[i].astype(F32)
    out[...] = total


def pack_kernel(key, value, out, sems):
    load = Loader(sems)
    rows = key.shape[0]
    copies = [load.start(key, out.at[pl.ds(0, rows), :]), load.start(value, out.at[pl.ds(rows, rows), :])]
    for copy in copies:
        copy.wait()


def call(kernel, out_shape, kinds, scratch=(), work=1000, limit=VMEM_LIMIT):
    place = {"s": pltpu.SMEM, "v": pltpu.VMEM, "a": pl.ANY, "h": pltpu.HBM}
    return pl.pallas_call(
        kernel,
        out_shape=out_shape,
        in_specs=[pl.BlockSpec(memory_space=place[kind]) for kind in kinds],
        out_specs=jax.tree.map(lambda _: pl.BlockSpec(memory_space=pltpu.VMEM), out_shape),
        scratch_shapes=list(scratch),
        compiler_params=pltpu.CompilerParams(vmem_limit_bytes=limit),
        cost_estimate=pl.CostEstimate(flops=work, bytes_accessed=1000, transcendentals=0),
    )


def body(query_rows, key_rows, value_rows, gate_rows, segment, w_out, cotangent):
    rows, width = query_rows.shape
    seg = segment.reshape(-1, rows)
    unit = w_out.shape[0]
    span = REACH * rows

    natural = np.arange(width)
    holder = natural // unit
    core, x, z, y = holder % NC, holder // NC % NX, holder // (NC * NX) % NZ, holder // (NC * NX * NZ)
    placed = (((core * NY + y) * NX + x) * NZ + z) * unit + natural % unit
    perm = jnp.asarray(np.eye(width, dtype=np.float32)[:, np.argsort(placed)], BF16)

    def like(*shape, dtype=BF16):
        return jax.ShapeDtypeStruct(shape, dtype)

    def scratch(*shape, dtype=BF16):
        return pltpu.VMEM(shape, dtype)

    seg_scratch = scratch(*seg.shape, dtype=jnp.int32)
    sems = lambda n: pltpu.SemaphoreType.DMA((n,))

    def pair(rows_of):
        return lax.all_gather(rows_of, "c", axis=0, tiled=True)

    def ahead(rows_of):
        return shift(rows_of, -2), shift(rows_of, -3, range(0, COUNT, 2))

    kv = call(pack_kernel, like(2 * rows, width), "hh", [sems(2)])(key_rows, value_rows)
    w_line = lax.all_to_all(
        jnp.broadcast_to(w_out[None], (NZ,) + w_out.shape), "z", 0, 0, tiled=True
    ).reshape(NZ * unit, width)
    kv_chip = shift(kv, 2)
    cot, k_pair, v_pair = pair(cotangent), pair(key_rows), pair(value_rows)
    kv_far = shift(kv, 3, range(1, COUNT, 2))
    q_chip, q_far = ahead(query_rows)
    kv_chip, kv_far, w_line, cot, k_pair, v_pair, q_chip, q_far = lax.optimization_barrier(
        (kv_chip, kv_far, w_line, cot, k_pair, v_pair, q_chip, q_far)
    )
    w_sub = lax.all_to_all(
        jnp.broadcast_to(w_line[None], (NY * NX,) + w_line.shape), PLANE, 0, 0, tiled=True
    ).reshape(CHIPS * unit, width)
    kv_cross = swap(kv_chip)
    memory = (kv, k_pair, v_pair, kv_chip, kv_cross, kv_far)

    normed, rstd, hidden = call(
        forward_kernel,
        (like(rows, width, dtype=F32), like(rows, 128, dtype=F32), like(rows, width)),
        "hhahhhhhhh",
        [
            seg_scratch, scratch(rows, width), scratch(span, width), scratch(span, width),
            scratch(rows, width), scratch(width, width), scratch(rows, width, dtype=F32), sems(12),
        ],
        limit=LARGE_LIMIT,
    )(seg, query_rows, *memory, gate_rows, perm)
    mine, sent = call(
        columns_kernel,
        (like(rows, CHIPS * unit, dtype=F32),) * 2,
        "vh",
        [scratch(CHIPS * unit, width), sems(4)],
    )(cot, w_sub)
    gate_grad, upper = call(upstream_kernel, (like(rows, width), like(rows, width)), "vvvvvv")(
        mine, pair(sent), normed, rstd, gate_rows, perm
    )

    u_chip, u_far = ahead(upper)
    u_pair = pair(upper)

    hidden, q_chip, q_far = lax.optimization_barrier((hidden, q_chip, q_far))
    w_part = call(weight_kernel, like(CHIPS * unit, width), "vv")(pair(hidden), cot)
    w_parts = lax.all_to_all(w_part.reshape(NY * NX, NZ * unit, width), PLANE, 0, 0, tiled=True)
    q_late, q_chip_late, _ = lax.optimization_barrier((query_rows, q_chip, u_pair))
    q_pair, q_chips = pair(q_late), pair(q_chip_late)
    w_parts, _ = lax.optimization_barrier((w_parts, u_pair))
    w_sum = call(sum_kernel, like(NZ * unit, width, dtype=F32), "v")(w_parts).reshape(NZ, unit, width)
    w_line = lax.all_to_all(w_sum, "z", 0, 0, tiled=True)
    upper_late, _ = lax.optimization_barrier((upper, w_sum))
    query_grad = call(
        query_kernel,
        like(rows, width),
        "a" * 9,
        [
            seg_scratch, scratch(rows, width), scratch(rows, width), scratch(span, width), scratch(span, width),
            sems(11),
        ],
        20_000_000_000,
        LARGE_LIMIT,
    )(seg, query_rows, upper_late, *memory)
    u_chip, _ = lax.optimization_barrier((u_chip, query_grad))
    u_chips = pair(u_chip)
    key_grad, value_grad = call(
        memory_kernel,
        (like(rows, width), like(rows, width)),
        "a" * 12,
        [seg_scratch, scratch(2 * rows, width), scratch(span, width), scratch(span, width), sems(10)],
        20_000_000_000,
    )(
        seg, kv, query_rows, q_pair, q_chip, q_chips, q_far,
        upper, u_pair, u_chip, u_chips, u_far,
    )
    w_line, _ = lax.optimization_barrier((w_line, key_grad))
    w_grad = call(sum_kernel, like(unit, width, dtype=F32), "v")(w_line)
    return (query_grad, key_grad, value_grad, gate_grad, w_grad)


def solution(mesh):
    fine = Mesh(
        mesh.devices.reshape(NY, NZ, NX, NC, mesh.devices.shape[1]), BLK + ("grp",)
    )
    every = ("grp",) + BLK
    rows = P(every, None)
    in_specs = (rows, rows, rows, rows, P("grp"), P(BLK, None), rows)
    return jax.shard_map(
        body, mesh=fine, in_specs=in_specs, out_specs=(rows,) * 5, check_vma=False
    )
```

```python
import jax
import jax.numpy as jnp
import numpy as np
from jax import lax
from jax.experimental import pallas as pl
from jax.experimental.pallas import tpu as pltpu
from jax.sharding import Mesh, PartitionSpec as P

DH = 128
REACH = 4
NY, NZ, NX, NC = 2, 8, 4, 2
COUNT = NY * NZ * NX * NC
BLK = ("y", "z", "x", "c")
PLANE = ("y", "x")
CHIPS = NY * NZ * NX
F32, BF16 = jnp.float32, jnp.bfloat16
SCALE = DH ** (-0.5)
VMEM_LIMIT = 20 * 1024 * 1024
LARGE_LIMIT = 58 * 1024 * 1024
HEADS_TOGETHER = 2


def shift(value, steps, sources=None):
    pairs = [(s, s + steps) for s in (sources or range(COUNT)) if 0 <= s + steps < COUNT]
    return lax.ppermute(value, BLK, pairs)


def ring(value, axis, size, steps):
    return lax.ppermute(value, axis, [(s, (s + steps) % size) for s in range(size)])


def swap(value):
    return ring(value, "c", NC, 1)


def dot(a, b, contract):
    return lax.dot_general(a, b, ((contract[:1], contract[1:]), ((), ())), preferred_element_type=F32)


def sigmoid(s):
    return 0.5 * jnp.tanh(0.5 * s) + 0.5


def position():
    y, z, x, c = (lax.axis_index(axis) for axis in BLK)
    return ((y * NZ + z) * NX + x) * NC + c, c


class Loader:
    def __init__(self, sems):
        self.sems, self.used = sems, 0

    def start(self, source, target):
        copy = pltpu.make_async_copy(source, target, self.sems.at[self.used])
        self.used += 1
        copy.start()
        return copy

    def choose(self, condition, source, otherwise, target):
        sem = self.sems.at[self.used]
        self.used += 1

        @pl.when(condition)
        def _():
            pltpu.make_async_copy(source, target, sem).start()

        @pl.when(jnp.logical_not(condition))
        def _():
            pltpu.make_async_copy(otherwise, target, sem).start()

        return pltpu.make_async_copy(source, target, sem)


def allowed_pairs(segs, block, direction):
    rows = segs.shape[1]
    last = segs.shape[0] - 1
    own = jnp.broadcast_to(segs[pl.ds(block, 1), :].astype(F32), (rows, rows)).T
    line = lax.broadcasted_iota(jnp.int32, (rows, rows), 0)
    lane = lax.broadcasted_iota(jnp.int32, (rows, rows), 1)
    masks = []
    for offset in range(REACH):
        there = jnp.clip(block + direction * offset, 0, last)
        mask = own == segs[pl.ds(there, 1), :].astype(F32)
        ahead = direction * (lane - line)
        if offset == 0:
            mask = mask & (ahead >= 0)
        if offset == REACH - 1:
            mask = mask & (ahead <= 0)
        masks.append(mask)
    return jnp.concatenate(masks, 1)


def head_groups(width):
    heads = [pl.ds(h * DH, DH) for h in range(width // DH)]
    return [heads[i:i + HEADS_TOGETHER] for i in range(0, len(heads), HEADS_TOGETHER)]


def load_memory(load, even, kv, k_pair, v_pair, chip, cross, far, kb, vb):
    rows = kv.shape[0] // 2
    copies = []
    for half, pair, buffer in ((0, k_pair, kb), (1, v_pair, vb)):
        part = pl.ds(half * rows, rows)
        slot = lambda o: buffer.at[pl.ds(o * rows, rows), :]
        copies.append(load.start(kv.at[part, :], slot(0)))
        copies.append(load.choose(even, cross.at[part, :], pair.at[pl.ds(0, rows), :], slot(1)))
        copies.append(load.start(chip.at[part, :], slot(2)))
        copies.append(load.choose(even, far.at[part, :], cross.at[part, :], slot(3)))
    return copies


def forward_kernel(
    seg, q, kv, k_pair, v_pair, chip, cross, far, gate, perm,
    normed_o, rstd_o, hidden_o,
    segs, qb, kb, vb, gb, pb, att, sems,
):
    load = Loader(sems)
    block, core = position()
    even = core == 0
    first = [load.start(seg, segs), load.start(q, qb)]
    first += load_memory(load, even, kv, k_pair, v_pair, chip, cross, far, kb, vb)
    later = [load.start(gate, gb), load.start(perm, pb)]
    for copy in first:
        copy.wait()
    width = qb.shape[1]
    allowed = allowed_pairs(segs, block, -1)
    for at in head_groups(width):
        scores = [dot(qb[:, h], kb[:, h], (1, 1)) * SCALE for h in at]
        weights = [jnp.where(allowed, s * sigmoid(s), 0.0).astype(BF16) for s in scores]
        for h, w in zip(at, weights):
            att[:, h] = dot(w, vb[:, h], (1, 0))
    attended = att[...]
    mean = jnp.mean(attended, axis=1, keepdims=True)
    centred = attended - mean
    rstd = lax.rsqrt(jnp.mean(centred * centred, axis=1, keepdims=True) + 1e-05)
    normed = centred * rstd
    normed_o[...] = normed
    rstd_o[...] = jnp.broadcast_to(rstd, rstd_o.shape)
    for copy in later:
        copy.wait()
    hidden = (normed * gb[...].astype(F32)).astype(BF16)
    hidden_o[...] = dot(hidden, pb[...], (1, 0)).astype(BF16)


def columns_kernel(cot, w_sub, mine_o, sent_o, wb, sems):
    load = Loader(sems)
    rows, half = mine_o.shape
    step = half // 4
    chunks = [pl.ds(i * step, step) for i in range(half // step)]
    copies = [load.start(w_sub.at[chunk, :], wb.at[chunk, :]) for chunk in chunks]
    core = position()[1]
    own = pl.ds(pl.multiple_of(core * rows, rows), rows)
    other = pl.ds(pl.multiple_of((1 - core) * rows, rows), rows)
    for chunk, copy in zip(chunks, copies):
        copy.wait()
        mine_o[:, chunk] = dot(cot[own, :], wb[chunk, :], (1, 1))
        sent_o[:, chunk] = dot(cot[other, :], wb[chunk, :], (1, 1))


def weight_kernel(hidden, cot, out):
    half = out.shape[0]
    columns = hidden[:, pl.ds(pl.multiple_of(position()[1] * half, half), half)]
    out[...] = dot(columns, cot[...], (0, 0)).astype(BF16)


def upstream_kernel(mine, both, normed, rstd, gate, perm, gate_o, upper_o):
    rows = mine.shape[0]
    own = mine[...]
    block, core = position()
    even = core == 0
    first = jnp.where(even, own, both[:rows])
    second = jnp.where(even, both[rows:], own)
    placed = jnp.concatenate([first, second], 1)
    high = placed.astype(BF16)
    low = (placed - high.astype(F32)).astype(BF16)
    hidden_grad = dot(high, perm[...], (1, 1)) + dot(low, perm[...], (1, 1))
    n = normed[...]
    gate_o[...] = (hidden_grad * n).astype(BF16)
    normed_grad = hidden_grad * gate[...].astype(F32)
    inner = (
        normed_grad
        - jnp.mean(normed_grad, axis=1, keepdims=True)
        - n * jnp.mean(normed_grad * n, axis=1, keepdims=True)
    )
    upper_o[...] = (rstd[:, :1] * inner).astype(BF16)


def query_kernel(
    seg, q, u, kv, k_pair, v_pair, chip, cross, far,
    query_o,
    segs, qb, ub, kb, vb, sems,
):
    load = Loader(sems)
    block, core = position()
    even = core == 0
    copies = [load.start(seg, segs), load.start(q, qb), load.start(u, ub)]
    copies += load_memory(load, even, kv, k_pair, v_pair, chip, cross, far, kb, vb)
    for copy in copies:
        copy.wait()
    width = query_o.shape[1]
    allowed = allowed_pairs(segs, block, -1)
    for at in head_groups(width):
        scores = [dot(qb[:, h], kb[:, h], (1, 1)) * SCALE for h in at]
        weight_grads = [dot(ub[:, h], vb[:, h], (1, 1)) for h in at]
        score_grads = []
        for s, weight_grad in zip(scores, weight_grads):
            sigma = sigmoid(s)
            grad = jnp.where(allowed, weight_grad * (sigma * (1.0 + s * (1.0 - sigma))), 0.0)
            score_grads.append(grad.astype(BF16))
        for h, grad in zip(at, score_grads):
            query_o[:, h] = (dot(grad, kb[:, h], (1, 0)) * SCALE).astype(BF16)


def memory_kernel(
    seg, kv, q, q_pair, q_chip, q_chips, q_far, u, u_pair, u_chip, u_chips, u_far,
    key_o, value_o,
    segs, kvb, qb, ub, sems,
):
    load = Loader(sems)
    block, core = position()
    even = core == 0
    rows, width = key_o.shape
    copies = [load.start(seg, segs), load.start(kv, kvb)]
    slot = lambda buffer, o: buffer.at[pl.ds(o * rows, rows), :]
    first, second = pl.ds(0, rows), pl.ds(rows, rows)
    for buffer, own, pair, chip, chips, far in (
        (qb, q, q_pair, q_chip, q_chips, q_far),
        (ub, u, u_pair, u_chip, u_chips, u_far),
    ):
        copies.append(load.start(own, slot(buffer, 0)))
        copies.append(load.choose(even, pair.at[second, :], chips.at[first, :], slot(buffer, 1)))
        copies.append(load.start(chip, slot(buffer, 2)))
        copies.append(load.choose(even, chips.at[second, :], far, slot(buffer, 3)))
    for copy in copies:
        copy.wait()
    allowed = allowed_pairs(segs, block, 1)
    for at in head_groups(width):
        scores = [dot(kvb[:rows, h], qb[:, h], (1, 1)) * SCALE for h in at]
        weight_grads = [dot(kvb[rows:, h], ub[:, h], (1, 1)) for h in at]
        weights, score_grads = [], []
        for s, weight_grad in zip(scores, weight_grads):
            sigma = sigmoid(s)
            weights.append(jnp.where(allowed, s * sigma, 0.0).astype(BF16))
            grad = jnp.where(allowed, weight_grad * (sigma * (1.0 + s * (1.0 - sigma))), 0.0)
            score_grads.append(grad.astype(BF16))
        for h, w, grad in zip(at, weights, score_grads):
            key_o[:, h] = (dot(grad, qb[:, h], (1, 0)) * SCALE).astype(BF16)
            value_o[:, h] = dot(w, ub[:, h], (1, 0)).astype(BF16)


def sum_kernel(parts, out):
    total = parts[0].astype(F32)
    for i in range(1, parts.shape[0]):
        total += parts[i].astype(F32)
    out[...] = total


def pack_kernel(key, value, out, sems):
    load = Loader(sems)
    rows = key.shape[0]
    copies = [load.start(key, out.at[pl.ds(0, rows), :]), load.start(value, out.at[pl.ds(rows, rows), :])]
    for copy in copies:
        copy.wait()


def call(kernel, out_shape, kinds, scratch=(), work=1000, limit=VMEM_LIMIT):
    place = {"s": pltpu.SMEM, "v": pltpu.VMEM, "a": pl.ANY, "h": pltpu.HBM}
    return pl.pallas_call(
        kernel,
        out_shape=out_shape,
        in_specs=[pl.BlockSpec(memory_space=place[kind]) for kind in kinds],
        out_specs=jax.tree.map(lambda _: pl.BlockSpec(memory_space=pltpu.VMEM), out_shape),
        scratch_shapes=list(scratch),
        compiler_params=pltpu.CompilerParams(vmem_limit_bytes=limit),
        cost_estimate=pl.CostEstimate(flops=work, bytes_accessed=1000, transcendentals=0),
    )


def body(query_rows, key_rows, value_rows, gate_rows, segment, w_out, cotangent):
    rows, width = query_rows.shape
    seg = segment.reshape(-1, rows)
    unit = w_out.shape[0]
    span = REACH * rows

    natural = np.arange(width)
    holder = natural // unit
    core, x, z, y = holder % NC, holder // NC % NX, holder // (NC * NX) % NZ, holder // (NC * NX * NZ)
    placed = (((core * NY + y) * NX + x) * NZ + z) * unit + natural % unit
    perm = jnp.asarray(np.eye(width, dtype=np.float32)[:, np.argsort(placed)], BF16)

    def like(*shape, dtype=BF16):
        return jax.ShapeDtypeStruct(shape, dtype)

    def scratch(*shape, dtype=BF16):
        return pltpu.VMEM(shape, dtype)

    seg_scratch = scratch(*seg.shape, dtype=jnp.int32)
    sems = lambda n: pltpu.SemaphoreType.DMA((n,))

    def pair(rows_of):
        return lax.all_gather(rows_of, "c", axis=0, tiled=True)

    def ahead(rows_of):
        return shift(rows_of, -2), shift(rows_of, -3, range(0, COUNT, 2))

    kv = call(pack_kernel, like(2 * rows, width), "hh", [sems(2)])(key_rows, value_rows)
    w_line = lax.all_to_all(
        jnp.broadcast_to(w_out[None], (NZ,) + w_out.shape), "z", 0, 0, tiled=True
    ).reshape(NZ * unit, width)
    kv_chip = shift(kv, 2)
    cot, k_pair, v_pair = pair(cotangent), pair(key_rows), pair(value_rows)
    kv_far = shift(kv, 3, range(1, COUNT, 2))
    q_late, k_pair, v_pair = lax.optimization_barrier((query_rows, k_pair, v_pair))
    q_chip, q_far = ahead(q_late)
    kv_chip, kv_far, w_line, cot, k_pair, v_pair, q_chip, q_far = lax.optimization_barrier(
        (kv_chip, kv_far, w_line, cot, k_pair, v_pair, q_chip, q_far)
    )
    w_sub = lax.all_to_all(
        jnp.broadcast_to(w_line[None], (NY * NX,) + w_line.shape), PLANE, 0, 0, tiled=True
    ).reshape(CHIPS * unit, width)
    kv_cross = swap(kv_chip)
    memory = (kv, k_pair, v_pair, kv_chip, kv_cross, kv_far)

    normed, rstd, hidden = call(
        forward_kernel,
        (like(rows, width, dtype=F32), like(rows, 128, dtype=F32), like(rows, width)),
        "hhahhhhhhh",
        [
            seg_scratch, scratch(rows, width), scratch(span, width), scratch(span, width),
            scratch(rows, width), scratch(width, width), scratch(rows, width, dtype=F32), sems(12),
        ],
        limit=LARGE_LIMIT,
    )(seg, query_rows, *memory, gate_rows, perm)
    mine, sent = call(
        columns_kernel,
        (like(rows, CHIPS * unit, dtype=F32),) * 2,
        "vh",
        [scratch(CHIPS * unit, width), sems(4)],
    )(cot, w_sub)
    gate_grad, upper = call(upstream_kernel, (like(rows, width), like(rows, width)), "vvvvvv")(
        mine, pair(sent), normed, rstd, gate_rows, perm
    )

    u_chip, u_far = ahead(upper)
    u_pair = pair(upper)

    hidden, q_chip, q_far = lax.optimization_barrier((hidden, q_chip, q_far))
    w_part = call(weight_kernel, like(CHIPS * unit, width), "vv")(pair(hidden), cot)
    w_parts = lax.all_to_all(w_part.reshape(NY * NX, NZ * unit, width), PLANE, 0, 0, tiled=True)
    q_late, q_chip_late, _ = lax.optimization_barrier((query_rows, q_chip, u_pair))
    q_pair, q_chips = pair(q_late), pair(q_chip_late)
    w_parts, _ = lax.optimization_barrier((w_parts, u_pair))
    w_sum = call(sum_kernel, like(NZ * unit, width, dtype=F32), "v")(w_parts).reshape(NZ, unit, width)
    w_line = lax.all_to_all(w_sum, "z", 0, 0, tiled=True)
    upper_late, _ = lax.optimization_barrier((upper, w_sum))
    query_grad = call(
        query_kernel,
        like(rows, width),
        "a" * 9,
        [
            seg_scratch, scratch(rows, width), scratch(rows, width), scratch(span, width), scratch(span, width),
            sems(11),
        ],
        20_000_000_000,
        LARGE_LIMIT,
    )(seg, query_rows, upper_late, *memory)
    u_chip, _ = lax.optimization_barrier((u_chip, query_grad))
    u_chips = pair(u_chip)
    key_grad, value_grad = call(
        memory_kernel,
        (like(rows, width), like(rows, width)),
        "a" * 12,
        [seg_scratch, scratch(2 * rows, width), scratch(span, width), scratch(span, width), sems(10)],
        20_000_000_000,
    )(
        seg, kv, query_rows, q_pair, q_chip, q_chips, q_far,
        upper, u_pair, u_chip, u_chips, u_far,
    )
    w_line, _ = lax.optimization_barrier((w_line, key_grad))
    w_grad = call(sum_kernel, like(unit, width, dtype=F32), "v")(w_line)
    return (query_grad, key_grad, value_grad, gate_grad, w_grad)


def solution(mesh):
    fine = Mesh(
        mesh.devices.reshape(NY, NZ, NX, NC, mesh.devices.shape[1]), BLK + ("grp",)
    )
    every = ("grp",) + BLK
    rows = P(every, None)
    in_specs = (rows, rows, rows, rows, P("grp"), P(BLK, None), rows)
    return jax.shard_map(
        body, mesh=fine, in_specs=in_specs, out_specs=(rows,) * 5, check_vma=False
    )
```
